32 devices in a mesh: dp: 8 (over z, core), tensor: 4 (over y, x).
Axes of the slice: x: 2, y: 2, z: 4, core: 2. Of those that a mesh axis runs over, the one named last changes fastest.
Arguments:
- hidden_in: bfloat16 [4096, 8192], P('dp', 'tensor'), may hold values from -6 to 6
- norm_gain: float32 [8192], P('tensor'), may hold values from 0.5 to 1.5
- key_weight: bfloat16 [8192, 512], P('tensor'), as said below
- value_weight: bfloat16 [8192, 512], P('tensor'), may hold values from -0.0625 to 0.0625
- queries: bfloat16 [4096, 4096], P('dp', 'tensor'), may hold values from -8 to 8
- segments: int32 [8, 512], P('dp'), may hold values from 0 to 3, never falling along the last dimension, each value on 1 to 256 neighbouring positions
- cotangent: bfloat16 [4096, 4096], P('dp', 'tensor'), may hold values from -6 to 6
Outputs:
- attn_out: bfloat16 [4096, 4096], P('dp', 'tensor')
- grad_hidden: bfloat16 [4096, 8192], P('dp', 'tensor')
- grad_queries: bfloat16 [4096, 4096], P('dp', 'tensor')
- grad_key_weight: float32 [8192, 512], P(('tensor', 'dp'))
- grad_value_weight: float32 [8192, 512], P(('tensor', 'dp'))
- grad_gain: float32 [8192], P(('tensor', 'dp'))
The draws below stay inside these ranges and needn't reach their ends.
Inputs may be any that keep to these rules, and one draw needn't show every extreme that they name: `segments`: segment numbers never fall along a row; each document has 1 to 256 tokens, one exactly 256. `key_weight`: entries have a standard deviation of about 8192^(-1/2) and lie within 6 such deviations.
All inputs are finite; a program needn't handle non-finite values.
Results may differ from the reference program's by a relative error of at most 0.035.
Values may be sent and summed in bfloat16 or wider, within the bound.
A program may use at most 64 MiB of HBM per device.

```python
import math
import jax
import jax.numpy as jnp
import numpy as np
from jax import lax

D = 8192
HQ = 32
KVH = 4
HD = 128
SEQ = 512
TOKENS = 4096
N_DP = 8


def column_scales(factor):
    place = jnp.arange(D).astype(jnp.float32) / D
    return 1.5 * jnp.exp(jnp.log(factor) * (place - 1.0))


def draw_key_weight(key, part):
    key = jax.random.fold_in(key, 7)
    noise = jax.random.normal(key, (D, KVH, HD), jnp.float32)
    weight = jnp.clip(noise, -6.0, 6.0)
    return (weight * D ** (-0.5)).reshape(D, KVH * HD).astype(jnp.bfloat16)


def draw_hidden_in(key, part):
    key = jax.random.fold_in(key, 13)
    key_base = jax.random.fold_in(key, 0)
    values = jax.random.normal(key_base, (TOKENS, D), jnp.float32)
    values = jnp.clip(values * column_scales(4.0)[None, :], -6.0, 6.0)
    return values.astype(jnp.bfloat16)


def draw_queries(key, part):
    key = jax.random.fold_in(key, 17)
    key_base = jax.random.fold_in(key, 0)
    values = jnp.clip(jax.random.normal(key_base, (TOKENS, HQ * HD), jnp.float32), -6.0, 6.0)
    return values.astype(jnp.bfloat16)


def block_scale(own_key, dims, cuts, smallest, high):
    factor_of, own = 1.0, jax.random.fold_in(own_key, 6)
    for axis_at, shards_of in cuts:
        draws = jnp.exp(jax.random.uniform(jax.random.fold_in(own, axis_at), (shards_of,), jnp.float32, smallest / len(cuts), high / len(cuts)))
        factor_of = factor_of * jnp.repeat(draws, dims[axis_at] // shards_of).reshape([-1 if axis == axis_at else 1 for axis in range(len(dims))])
    return factor_of


def length_profile(count, total, bound, lean):
    weights = [(1 << 20) // math.isqrt(rank ** lean) + 1 for rank in range(2, count + 1)]
    spare, holding = total - bound - (count - 1), [1] * (count - 1)
    while spare > 0:
        candidates = [i for i in range(count - 1) if holding[i] < bound]
        whole, budget = sum([weights[i] for i in candidates]), spare
        for i in candidates:
            more = min(bound - holding[i], max(1, budget * weights[i] // whole), spare)
            holding[i] = holding[i] + more
            spare = spare - more
    return np.array([bound] + holding)


def ragged(rng, count, total, most, slope):
    if count == 2:
        one = jax.random.randint(rng, (), max(1, total - most), min(most, total - 1) + 1)
        return jnp.stack([one, total - one])
    lengths = jnp.asarray(length_profile(count, total, most, slope), jnp.int32)
    pairs = (count - 1) // 2
    donor, sink = lengths[1:1 + 2 * pairs:2], lengths[2:2 + 2 * pairs:2]
    slack = jnp.minimum(donor - 1, most - sink)
    moved = jax.random.randint(jax.random.fold_in(rng, 1), (pairs,), 0, 1 << 20) % (slack + 1)
    lengths = lengths.at[1:1 + 2 * pairs:2].set(donor - moved).at[2:2 + 2 * pairs:2].set(sink + moved)
    return lengths[jax.random.permutation(jax.random.fold_in(rng, 2), count)]


def centred(own_key, shape, deviation, limit, shards=(), kind=jnp.bfloat16):
    array = jax.random.normal(own_key, shape, jnp.float32) * deviation
    if len(shards) > 0:
        array = block_scale(own_key, shape, shards, -0.22, 0.18) * array
    return jnp.clip(array, min=-limit, max=limit).astype(kind)


def setup_inputs(seed: int = 0) -> dict:
    streams_of = jax.random.split(jax.random.key(seed), 8)
    hidden_in = draw_hidden_in(jax.random.fold_in(streams_of[7], 71), 0)
    norm_gain = jnp.clip(1.0 + 0.1 * jax.random.normal(streams_of[1], (D,), jnp.float32), 0.5, 1.5)
    key_weight = draw_key_weight(jax.random.fold_in(streams_of[7], 71), 0)
    value_weight = centred(streams_of[3], (D, KVH * HD), D ** -0.5, 0.0625, ((0, 4),))
    queries = draw_queries(jax.random.fold_in(streams_of[7], 71), 0)
    segments = jax.vmap(lambda own: jnp.searchsorted(jnp.cumsum(ragged(own, 4, SEQ, SEQ // 2, 0)), jnp.arange(SEQ), side="right"))(jax.random.split(streams_of[5], N_DP)).reshape((N_DP, SEQ)).astype(jnp.int32)
    cotangent = centred(streams_of[6], (TOKENS, HQ * HD), 1.0, 6.0, ((0, 8), (1, 4)))
    return {"hidden_in": hidden_in, "norm_gain": norm_gain, "key_weight": key_weight, "value_weight": value_weight, "queries": queries, "segments": segments, "cotangent": cotangent}


ROPE_BASE = 500000.0

def angles(pos, head_size, ndim):
    half = head_size // 2
    freq = ROPE_BASE ** (-(jnp.arange(half).astype(jnp.float32) * 2.0 / head_size))
    angle = pos[:, None] * freq[None, :]
    shape = (pos.shape[0],) + (1,) * (ndim - 2) + (half,)
    return (jnp.cos(angle).reshape(shape), jnp.sin(angle).reshape(shape))

def rotate(vec, pos, sign):
    half = vec.shape[-1] // 2
    cosine, sine = angles(pos, vec.shape[-1], vec.ndim)
    first = vec[..., :half]
    second = vec[..., half:]
    return jnp.concatenate([first * cosine - sign * second * sine, second * cosine + sign * first * sine], axis=-1)

def row_layout(seg):
    rows = seg.shape[0]
    index = jnp.arange(rows).astype(jnp.int32)
    same = seg[:, None] == seg[None, :]
    start = lax.optimization_barrier(jnp.min(jnp.where(same, index[None, :], rows), axis=1))
    pos = (index - start).astype(jnp.float32)
    allowed = same & (index[None, :] <= index[:, None])
    return (pos, allowed)

def one_row(hidden_in, norm_gain, key_weight, value_weight, queries, seg, cotangent):
    rows = hidden_in.shape[0]
    group = HQ // KVH
    scale = 1.0 / HD ** 0.5
    in_float = hidden_in.astype(jnp.float32)
    inv_rms = lax.rsqrt(lax.optimization_barrier(jnp.sum(in_float * in_float, axis=1)) / D + 1e-05)
    unit = in_float * inv_rms[:, None]
    normed = (unit * norm_gain[None, :]).astype(jnp.bfloat16)
    keys = jnp.dot(normed, key_weight, preferred_element_type=jnp.float32).astype(jnp.bfloat16)
    values = jnp.dot(normed, value_weight, preferred_element_type=jnp.float32).astype(jnp.bfloat16)
    pos, allowed = row_layout(seg)
    query_four = queries.astype(jnp.float32).reshape(rows, KVH, group, HD)
    q_rot = rotate(query_four, pos, 1.0).astype(jnp.bfloat16).astype(jnp.float32)
    k_rot = rotate(keys.astype(jnp.float32).reshape(rows, KVH, HD), pos, 1.0).astype(jnp.bfloat16).astype(jnp.float32)
    val_three = values.astype(jnp.float32).reshape(rows, KVH, HD)
    scores = jnp.einsum('qcrd,kcd->crqk', q_rot, k_rot) * scale
    scores = jnp.where(allowed[None, None], scores, -1e+30)
    top = lax.optimization_barrier(jnp.max(scores, axis=-1, keepdims=True))
    expo = jnp.exp(scores - top)
    probs = (expo / lax.optimization_barrier(jnp.sum(expo, axis=-1, keepdims=True))).astype(jnp.bfloat16).astype(jnp.float32)
    attn_out = jnp.einsum('crqk,kcd->qcrd', probs, val_three).astype(jnp.bfloat16).reshape(rows, HQ * HD)
    cot_four = cotangent.astype(jnp.float32).reshape(rows, KVH, group, HD)
    d_probs = jnp.einsum('qcrd,kcd->crqk', cot_four, val_three)
    delta = lax.optimization_barrier(jnp.sum(probs * d_probs, axis=-1, keepdims=True))
    d_scores = (probs * (d_probs - delta) * scale).astype(jnp.bfloat16).astype(jnp.float32)
    d_qrot = jnp.einsum('crqk,kcd->qcrd', d_scores, k_rot)
    grad_queries = rotate(d_qrot, pos, -1.0).astype(jnp.bfloat16).reshape(rows, HQ * HD)
    d_krot = jnp.einsum('crqk,qcrd->kcd', d_scores, q_rot)
    d_keys = rotate(d_krot, pos, -1.0).astype(jnp.bfloat16).reshape(rows, KVH * HD)
    d_values = jnp.einsum('crqk,qcrd->kcd', probs, cot_four).astype(jnp.bfloat16).reshape(rows, KVH * HD)
    d_normed = jnp.dot(d_keys, key_weight.T, preferred_element_type=jnp.float32) + jnp.dot(d_values, value_weight.T, preferred_element_type=jnp.float32)
    grad_key = jnp.dot(normed.T, d_keys, preferred_element_type=jnp.float32)
    grad_value = jnp.dot(normed.T, d_values, preferred_element_type=jnp.float32)
    grad_gain = lax.optimization_barrier(jnp.sum(d_normed * unit, axis=0))
    d_unit = d_normed * norm_gain[None, :]
    corr = lax.optimization_barrier(jnp.sum(d_unit * unit, axis=1)) / D
    grad_hidden = (inv_rms[:, None] * (d_unit - unit * corr[:, None])).astype(jnp.bfloat16)
    return (attn_out, grad_hidden, grad_queries, grad_key, grad_value, grad_gain)

def reference(hidden_in, norm_gain, key_weight, value_weight, queries, segments, cotangent):
    nrows = segments.shape[0]
    hidden_rows = hidden_in.reshape(nrows, SEQ, D)
    query_rows = queries.reshape(nrows, SEQ, HQ * HD)
    cot_rows = cotangent.reshape(nrows, SEQ, HQ * HD)

    def step(carry, item):
        hid, qry, seg, cot = item
        attn_out, grad_hidden, grad_queries, grad_key, grad_value, grad_gain = one_row(hid, norm_gain, key_weight, value_weight, qry, seg, cot)
        carry = (carry[0] + grad_key, carry[1] + grad_value, carry[2] + grad_gain)
        return (carry, (attn_out, grad_hidden, grad_queries))
    start = (jnp.zeros((D, KVH * HD), jnp.float32), jnp.zeros((D, KVH * HD), jnp.float32), jnp.zeros((D,), jnp.float32))
    sums, outs = lax.scan(step, start, (hidden_rows, query_rows, segments, cot_rows))
    attn_out = outs[0].reshape(nrows * SEQ, HQ * HD)
    grad_hidden = outs[1].reshape(nrows * SEQ, D)
    grad_queries = outs[2].reshape(nrows * SEQ, HQ * HD)
    return (attn_out, grad_hidden, grad_queries, sums[0], sums[1], sums[2])
```

```python
import functools

import jax
import jax.numpy as jnp
import numpy as np
from jax import lax
from jax.experimental import pallas as pl
from jax.experimental.pallas import tpu as pltpu
from jax.sharding import PartitionSpec as P

D = 8192
HQ = 32
KVH = 4
HD = 128


ROPE_BASE = 500000.0


def angles(pos, head_size, ndim):
    half = head_size // 2
    freq = ROPE_BASE ** (-(jnp.arange(half).astype(jnp.float32) * 2.0 / head_size))
    angle = pos[:, None] * freq[None, :]
    shape = (pos.shape[0],) + (1,) * (ndim - 2) + (half,)
    return (jnp.cos(angle).reshape(shape), jnp.sin(angle).reshape(shape))


def rotate(vec, pos, sign):
    half = vec.shape[-1] // 2
    cosine, sine = angles(pos, vec.shape[-1], vec.ndim)
    first = vec[..., :half]
    second = vec[..., half:]
    return jnp.concatenate(
        [first * cosine - sign * second * sine, second * cosine + sign * first * sine], axis=-1
    )


def row_layout(seg):
    rows = seg.shape[0]
    index = jnp.arange(rows)
    same = seg[:, None] == seg[None, :]
    start = jnp.min(jnp.where(same, index[None, :], rows), axis=1)
    pos = (index - start).astype(jnp.float32)
    allowed = same & (index[None, :] <= index[:, None])
    return (pos, allowed)


def plain_body(hidden_in, norm_gain, key_weight, value_weight, queries, segments, cotangent):
    rows = hidden_in.shape[0]
    width = key_weight.shape[1]
    group = HQ // KVH
    scale = 1.0 / HD**0.5
    tens_size = lax.axis_size("tensor")
    tens_index = lax.axis_index("tensor")
    local_heads = queries.shape[1] // HD
    kv_count = max(local_heads // group, 1)
    repeat = min(local_heads, group)
    kv_first = tens_index * local_heads // group
    sharers = max(tens_size // KVH, 1)
    in_float = hidden_in.astype(jnp.float32)
    square_sum = lax.psum(jnp.sum(in_float * in_float, axis=1), "tensor")
    inv_rms = lax.rsqrt(square_sum / D + 1e-05)
    unit = in_float * inv_rms[:, None]
    normed = (unit * norm_gain[None, :]).astype(jnp.bfloat16)
    partial_value = jnp.stack(
        [
            jnp.dot(normed, key_weight, preferred_element_type=jnp.float32),
            jnp.dot(normed, value_weight, preferred_element_type=jnp.float32),
        ],
        axis=1,
    )
    kv_both = lax.psum(partial_value.reshape(rows, 2 * width), "tensor").astype(jnp.bfloat16)
    kv_heads = kv_both.reshape(rows, 2, KVH, HD)
    key_local = lax.dynamic_slice_in_dim(kv_heads[:, 0], kv_first, kv_count, 1)
    value_local = lax.dynamic_slice_in_dim(kv_heads[:, 1], kv_first, kv_count, 1)
    pos, allowed = row_layout(segments[0])
    query_four = queries.reshape(rows, kv_count, repeat, HD)
    q_rot = rotate(query_four.astype(jnp.float32), pos, 1.0).astype(jnp.bfloat16)
    k_rot = rotate(key_local.astype(jnp.float32), pos, 1.0).astype(jnp.bfloat16)
    scores = jnp.einsum("qcrd,kcd->crqk", q_rot, k_rot, preferred_element_type=jnp.float32) * scale
    scores = jnp.where(allowed[None, None], scores, -1e30)
    top = jnp.max(scores, axis=-1, keepdims=True)
    expo = jnp.exp(scores - top)
    probs = (expo / jnp.sum(expo, axis=-1, keepdims=True)).astype(jnp.bfloat16)
    attn_out = (
        jnp.einsum("crqk,kcd->qcrd", probs, value_local, preferred_element_type=jnp.float32)
        .astype(jnp.bfloat16)
        .reshape(rows, local_heads * HD)
    )
    cot_four = cotangent.reshape(rows, kv_count, repeat, HD)
    d_probs = jnp.einsum(
        "qcrd,kcd->crqk", cot_four, value_local, preferred_element_type=jnp.float32
    )
    prob_float = probs.astype(jnp.float32)
    delta = jnp.sum(prob_float * d_probs, axis=-1, keepdims=True)
    d_scores = (prob_float * (d_probs - delta) * scale).astype(jnp.bfloat16)
    d_qrot = jnp.einsum("crqk,kcd->qcrd", d_scores, k_rot, preferred_element_type=jnp.float32)
    grad_queries = rotate(d_qrot, pos, -1.0).astype(jnp.bfloat16).reshape(rows, local_heads * HD)
    d_krot = jnp.einsum("crqk,qcrd->kcd", d_scores, q_rot, preferred_element_type=jnp.float32)
    d_key_part = rotate(d_krot, pos, -1.0)
    d_value_part = jnp.einsum("crqk,qcrd->kcd", probs, cot_four, preferred_element_type=jnp.float32)
    grad_part = jnp.stack([d_key_part, d_value_part], axis=1)
    gathered = lax.all_gather(grad_part.astype(jnp.bfloat16), "tensor", axis=2, tiled=True).astype(
        grad_part.dtype
    )
    summed = jnp.sum(gathered.reshape(rows, 2, KVH, sharers, HD), axis=3)
    kv_grad = summed.astype(jnp.bfloat16).reshape(rows, 2, width)
    d_keys = kv_grad[:, 0]
    d_values = kv_grad[:, 1]
    d_normed = jnp.dot(d_keys, key_weight.T, preferred_element_type=jnp.float32) + jnp.dot(
        d_values, value_weight.T, preferred_element_type=jnp.float32
    )
    key_term = jnp.dot(normed.T, d_keys, preferred_element_type=jnp.float32)
    value_term = jnp.dot(normed.T, d_values, preferred_element_type=jnp.float32)
    gain_term = jnp.sum(d_normed * unit, axis=0)
    grad_key, grad_value, grad_gain = (
        lax.psum_scatter(
            key_term.astype(jnp.bfloat16), "dp", scatter_dimension=0, tiled=True
        ).astype(jnp.float32),
        lax.psum_scatter(
            value_term.astype(jnp.bfloat16), "dp", scatter_dimension=0, tiled=True
        ).astype(jnp.float32),
        lax.psum_scatter(
            gain_term.astype(jnp.bfloat16), "dp", scatter_dimension=0, tiled=True
        ).astype(jnp.float32),
    )
    d_unit = d_normed * norm_gain[None, :]
    corr = lax.psum(jnp.sum(d_unit * unit, axis=1), "tensor") / D
    grad_hidden = (inv_rms[:, None] * (d_unit - unit * corr[:, None])).astype(jnp.bfloat16)
    return (attn_out, grad_hidden, grad_queries, grad_key, grad_value, grad_gain)


ZS = 4
TS = 4
ROWS = 512
FEAT = 2048
BLK = 128
NB = ROWS // BLK
HEADS = HQ // TS
GH = 4
KV = 2 * HD
SH = FEAT // (2 * ZS)
KV_SEND = jnp.float32
MESH = pl.DeviceIdType.MESH
F32 = jnp.float32
BF16 = jnp.bfloat16


def dot_nn(a, b):
    return lax.dot_general(a, b, (((1,), (0,)), ((), ())), preferred_element_type=F32)


def dot_nt(a, b):
    return lax.dot_general(a, b, (((1,), (1,)), ((), ())), preferred_element_type=F32)


def dot_tn(a, b):
    return lax.dot_general(a, b, (((0,), (0,)), ((), ())), preferred_element_type=F32)


def eye_mask():
    return lax.broadcasted_iota(jnp.int32, (BLK, BLK), 0) == lax.broadcasted_iota(
        jnp.int32, (BLK, BLK), 1
    )


def col_to_row(col):
    return jnp.sum(jnp.where(eye_mask(), col, 0.0), axis=0, keepdims=True)


def row_to_col(row):
    return jnp.sum(jnp.where(eye_mask(), row, 0.0), axis=1, keepdims=True)


def swap_halves(vec):
    return pltpu.roll(vec, HD // 2, vec.ndim - 1)


def fused_kernel(
    hid_h, gain_v, kw_h, vw_h, q_h, seg_v, cot_h, freq_v,
    ao_h, gh_h, gq_h, gk_h, gv_h, gg_v,
    hid, w4, qs, cs, qr, cosv, sinv, segc, invc, normed, nt,
    ss, sbuf, rbuf, own_kv, krot, vals, dk_acc, dv_acc, ao, gq,
    dkv, du, corr_acc, cc, gsend, grecv,
    csend, crecv, own, zsend, zfl, zfr, gkv, gvv, gh,
    in_sem, out_sem, ss_s, ss_r, kv_s, kv_r, ag_s, ag_r, co_s, co_r,
    ga_s, ga_r, cx_s, cx_r, zs_s, zl_r, zr_r,
):
    dp = lax.axis_index("dp")
    t = lax.axis_index("tensor")
    z = dp // 2
    core = dp % 2
    other = 1 - core
    dp_other = dp + 1 - 2 * core
    peers = [t, t + 1 - 2 * (t % 2), (t + 2) % 4, 3 - t]

    def remote(src, dst, ssem, rsem, dev):
        return pltpu.make_async_remote_copy(
            src_ref=src, dst_ref=dst, send_sem=ssem, recv_sem=rsem,
            device_id=dev, device_id_type=MESH,
        )

    barrier = pltpu.get_barrier_semaphore()
    for p in range(1, 4):
        pl.semaphore_signal(barrier, inc=1, device_id=(dp, peers[p]), device_id_type=MESH)
    for k in range(1, 2 * ZS):
        pl.semaphore_signal(
            barrier, inc=1, device_id=((dp + k) % (2 * ZS), t), device_id_type=MESH
        )

    loads = [pltpu.make_async_copy(hid_h, hid, in_sem.at[0])]
    q_loads = [
        pltpu.make_async_copy(q_h.at[:, pl.ds(h * HD, HD)], qs.at[h], in_sem.at[1 + h])
        for h in range(HEADS)
    ]
    w_loads = []
    for h in range(KVH):
        w_loads.append(pltpu.make_async_copy(
            kw_h.at[:, pl.ds(h * HD, HD)], w4.at[h, :, pl.ds(0, HD)], in_sem.at[9 + 2 * h]))
        w_loads.append(pltpu.make_async_copy(
            vw_h.at[:, pl.ds(h * HD, HD)], w4.at[h, :, pl.ds(HD, HD)], in_sem.at[10 + 2 * h]))
    c_loads = [
        pltpu.make_async_copy(cot_h.at[:, pl.ds(h * HD, HD)], cs.at[h], in_sem.at[17 + h])
        for h in range(HEADS)
    ]
    for c in loads + q_loads + w_loads + c_loads:
        c.start()

    loads[0].wait()
    for b in range(NB):
        x = hid[pl.ds(b * BLK, BLK), :].astype(F32)
        ss[0, :, pl.ds(b * BLK, BLK)] = jnp.broadcast_to(
            col_to_row(jnp.sum(x * x, axis=1, keepdims=True)), (8, BLK)
        )
    pl.semaphore_wait(barrier, 3 + 2 * ZS - 1)

    def ss_copy(p):
        return remote(ss.at[0], ss.at[p], ss_s.at[p - 1], ss_r.at[p - 1], (dp, peers[p]))

    for p in range(1, 4):
        ss_copy(p).start()

    segr = seg_v[...].astype(F32)
    for b in range(NB):
        rows = pl.ds(b * BLK, BLK)
        col = row_to_col(segr[:, b * BLK:(b + 1) * BLK])
        segc[rows, :] = col
        start = jnp.sum(jnp.where(segr < col, 1.0, 0.0), axis=1, keepdims=True)
        index = lax.broadcasted_iota(jnp.int32, (BLK, 1), 0).astype(F32) + float(b * BLK)
        angle = (index - start) * freq_v[...]
        lane = lax.broadcasted_iota(jnp.int32, (BLK, HD), 1)
        cosv[rows, :] = jnp.cos(angle)
        sinv[rows, :] = jnp.where(lane < HD // 2, -1.0, 1.0) * jnp.sin(angle)
    for c in q_loads:
        c.wait()

    def rot_query(h, carry):
        v = qs[h].astype(F32)
        qr[h] = (v * cosv[...] + swap_halves(v) * sinv[...]).astype(BF16)
        return carry

    lax.fori_loop(0, HEADS, rot_query, 0)

    for p in range(1, 4):
        ss_copy(p).wait_recv()
    total = ss[0, 0:1, :] + ss[1, 0:1, :] + ss[2, 0:1, :] + ss[3, 0:1, :]
    inv_row = lax.rsqrt(total / D + 1e-05)
    for b in range(NB):
        invc[pl.ds(b * BLK, BLK), :] = row_to_col(inv_row[:, b * BLK:(b + 1) * BLK])
    for c in w_loads:
        c.wait()

    def kv_copy(b, p):
        return remote(
            sbuf.at[b, p - 1], rbuf.at[b, p - 1], kv_s.at[b, p - 1], kv_r.at[b, p - 1],
            (dp, peers[p]),
        )

    for b in range(NB):
        rows = pl.ds(b * BLK, BLK)
        unit = hid[rows, :].astype(F32) * invc[rows, :]
        normed[rows, :] = (unit * gain_v[...]).astype(BF16)
        for p in (3, 1, 2, 0):
            part = dot_nn(normed[rows, :], w4[peers[p]])
            if p == 0:
                own_kv[b] = part
            else:
                sbuf[b, p - 1] = part.astype(KV_SEND)
                kv_copy(b, p).start()
    for b in range(NB):
        rows = pl.ds(b * BLK, BLK)
        nt[:, pl.ds(b * BLK, BLK)] = normed[rows, :].astype(F32).T.astype(BF16)
    for c in c_loads:
        c.wait()

    dk_acc[...] = jnp.zeros_like(dk_acc)
    dv_acc[...] = jnp.zeros_like(dv_acc)
    scale = 1.0 / HD**0.5

    def ag_copy(part, p):
        rows = pl.ds(0, BLK) if part == 0 else pl.ds(BLK, ROWS - BLK)
        return remote(
            dkv.at[t, rows], dkv.at[t, rows], ag_s.at[part, p - 1], ag_r.at[part, p - 1],
            (dp, peers[p]),
        )

    def ag_wait(part, p):
        rows = pl.ds(0, BLK) if part == 0 else pl.ds(BLK, ROWS - BLK)
        remote(
            dkv.at[peers[p], rows], dkv.at[peers[p], rows], ag_s.at[part, p - 1],
            ag_r.at[part, p - 1], (dp, peers[p]),
        ).wait_recv()

    def finish_grads(part):
        rows = pl.ds(0, BLK) if part == 0 else pl.ds(BLK, ROWS - BLK)
        dk = dk_acc[rows, :]
        dkv[t, rows, pl.ds(0, HD)] = (
            dk * cosv[rows, :] - swap_halves(dk) * sinv[rows, :]
        ).astype(BF16)
        dkv[t, rows, pl.ds(HD, HD)] = dv_acc[rows, :].astype(BF16)
        for p in (3, 1, 2):
            ag_copy(part, p).start()

    for b in range(NB):
        rows = pl.ds(b * BLK, BLK)
        low = max(0, b - 2) * BLK
        width = (b + 1) * BLK - low
        window = pl.ds(low, width)
        for p in range(1, 4):
            kv_copy(b, p).wait_recv()
        both = own_kv[b]
        for p in range(1, 4):
            both = both + rbuf[b, p - 1].astype(F32)
        both = both.astype(BF16)
        key = both[:, :HD].astype(F32)
        krot[rows, :] = (key * cosv[rows, :] + swap_halves(key) * sinv[rows, :]).astype(BF16)
        vals[rows, :] = both[:, HD:]
        q_index = lax.broadcasted_iota(jnp.int32, (BLK, width), 0) + b * BLK
        k_index = lax.broadcasted_iota(jnp.int32, (BLK, width), 1) + low
        same = segc[rows, :] == segr[:, low:low + width]
        bias = jnp.where(same & (k_index <= q_index), 0.0, -1e30)

        def group(g, carry):
            heads = pl.ds(g * GH, GH)
            qg = qr[heads, rows, :].reshape(GH * BLK, HD)
            cg = cs[heads, rows, :].reshape(GH * BLK, HD)
            kwin = krot[window, :]
            vwin = vals[window, :]
            s = dot_nt(qg, kwin).reshape(GH, BLK, width) * scale + bias[None]
            e = jnp.exp(s - jnp.max(s, axis=-1, keepdims=True))
            pb = (e * (1.0 / jnp.sum(e, axis=-1, keepdims=True))).astype(BF16)
            pf = pb.astype(F32)
            pb = pb.reshape(GH * BLK, width)
            ao[heads, rows, :] = dot_nn(pb, vwin).astype(BF16).reshape(GH, BLK, HD)
            dpr = dot_nt(cg, vwin).reshape(GH, BLK, width)
            delta = jnp.sum(pf * dpr, axis=-1, keepdims=True)
            ds = (pf * (dpr - delta) * scale).astype(BF16).reshape(GH * BLK, width)
            dq = dot_nn(ds, kwin).reshape(GH, BLK, HD)
            gq[heads, rows, :] = (
                dq * cosv[rows, :][None] - swap_halves(dq) * sinv[rows, :][None]
            ).astype(BF16)
            dk_acc[window, :] += dot_tn(ds, qg)
            dv_acc[window, :] += dot_tn(pb, cg)
            return carry

        lax.fori_loop(0, HEADS // GH, group, 0)
        if b == 2:
            finish_grads(0)
    finish_grads(1)

    outs = []
    for h in range(HEADS):
        outs.append(pltpu.make_async_copy(ao.at[h], ao_h.at[:, pl.ds(h * HD, HD)], out_sem.at[h]))
        outs.append(pltpu.make_async_copy(
            gq.at[h], gq_h.at[:, pl.ds(h * HD, HD)], out_sem.at[HEADS + h]))
    for c in outs:
        c.start()

    def cx_copy(p, zt):
        return remote(
            csend.at[p, zt], crecv.at[p, zt], cx_s.at[p, zt], cx_r.at[p, zt], (dp_other, t)
        )

    def partials(p):
        for zt in range(ZS):
            far = nt[pl.ds((2 * zt + other) * SH, SH), :]
            csend[p, zt] = dot_nn(far, dkv[peers[p]]).astype(BF16)
            cx_copy(p, zt).start()
        for zt in range(ZS):
            near = nt[pl.ds((2 * zt + core) * SH, SH), :]
            own[p, zt] = dot_nn(near, dkv[peers[p]])

    def pair_sums(p):
        for zt in (3, 0, 2, 1):
            cx_copy(p, zt).wait_recv()
            own[p, zt] = own[p, zt] + crecv[p, zt].astype(F32)

    def right_copy(p, zt):
        return remote(
            zsend.at[p, zt], zfl.at[p, zt], zs_s.at[p, zt], zl_r.at[p, zt], ((dp + 2) % (2 * ZS), t)
        )

    def left_copy(p, zt):
        return remote(
            zsend.at[p, zt], zfr.at[p, zt], zs_s.at[p, zt], zr_r.at[p, zt], ((dp + 2 * ZS - 2) % (2 * ZS), t)
        )

    def end_sends(p):
        @pl.when(z == 0)
        def _():
            for zt in range(ZS - 1, 0, -1):
                zsend[p, zt] = own[p, zt].astype(BF16)
                right_copy(p, zt).start()

        @pl.when(z == ZS - 1)
        def _():
            for zt in range(ZS - 1):
                zsend[p, zt] = own[p, zt].astype(BF16)
                left_copy(p, zt).start()

    def middle_sends(p):
        for k in range(ZS - 1):
            zt = ZS - 1 - k

            @pl.when((z > 0) & (z < zt))
            def _():
                right_copy(p, zt).wait_recv()
                zsend[p, zt] = (own[p, zt] + zfl[p, zt].astype(F32)).astype(BF16)
                right_copy(p, zt).start()

            @pl.when((z < ZS - 1) & (z > k))
            def _():
                left_copy(p, k).wait_recv()
                zsend[p, k] = (own[p, k] + zfr[p, k].astype(F32)).astype(BF16)
                left_copy(p, k).start()

    partials(0)
    pair_sums(0)
    end_sends(0)
    for p in range(1, 4):
        ag_wait(0, p)
        ag_wait(1, p)
        partials(p)
    for p in range(1, 4):
        pair_sums(p)
        end_sends(p)

    corr_acc[...] = jnp.zeros_like(corr_acc)

    def feature_chunk(f, carry):
        cols = pl.ds(pl.multiple_of(f * SH, SH), SH)
        dn = dot_nt(dkv[0], w4[0, cols, :])
        for h in range(1, KVH):
            dn = dn + dot_nt(dkv[h], w4[h, cols, :])
        unit = hid[:, cols].astype(F32) * invc[...]
        gsend[f] = jnp.sum((dn * unit).reshape(ROWS // 8, 8, SH), axis=0)
        dun = dn * gain_v[:, cols]
        du[:, cols] = dun
        w = dun * unit
        corr_acc[...] += w[:, :128] + w[:, 128:]
        return carry

    lax.fori_loop(0, 2 * ZS, feature_chunk, 0)
    for b in range(NB):
        rows = pl.ds(b * BLK, BLK)
        cc[0, :, rows] = jnp.broadcast_to(
            col_to_row(jnp.sum(corr_acc[rows, :], axis=1, keepdims=True)), (8, BLK)
        )

    def cc_copy(p):
        return remote(cc.at[0], cc.at[p], co_s.at[p - 1], co_r.at[p - 1], (dp, peers[p]))

    def gain_copy(k):
        to = (dp + k) % (2 * ZS)
        return remote(gsend.at[to], grecv.at[k], ga_s.at[k], ga_r.at[k], (to, t))

    for p in range(1, 4):
        cc_copy(p).start()
    for k in range(1, 2 * ZS):
        gain_copy(k).start()

    middle_sends(0)
    for p in range(1, 4):
        cc_copy(p).wait_recv()
    corr_row = (cc[0, 0:1, :] + cc[1, 0:1, :] + cc[2, 0:1, :] + cc[3, 0:1, :]) / D
    for b in range(NB):
        rows = pl.ds(b * BLK, BLK)
        corr = row_to_col(corr_row[:, b * BLK:(b + 1) * BLK])
        inv = invc[rows, :]
        unit = hid[rows, :].astype(F32) * inv
        gh[rows, :] = (inv * (du[rows, :] - unit * corr)).astype(BF16)
    gh_out = pltpu.make_async_copy(gh, gh_h, out_sem.at[2 * HEADS])
    gh_out.start()

    for p in range(1, 4):
        middle_sends(p)

    for k in range(1, 2 * ZS):
        gain_copy(k).wait_recv()
    gain_sum = gsend[dp]
    for k in range(1, 2 * ZS):
        gain_sum = gain_sum + grecv[k]
    gg_v[...] = jnp.sum(gain_sum, axis=0, keepdims=True)

    for p in range(4):
        for zt in range(ZS):
            @pl.when(z == zt)
            def _():
                res = own[p, zt]
                if zt > 0:
                    right_copy(p, zt).wait_recv()
                    res = res + zfl[p, zt].astype(F32)
                if zt < ZS - 1:
                    left_copy(p, zt).wait_recv()
                    res = res + zfr[p, zt].astype(F32)
                cols = pl.ds(pl.multiple_of(peers[p] * HD, HD), HD)
                gkv[:, cols] = res[:, :HD]
                gvv[:, cols] = res[:, HD:]
    gk_out = pltpu.make_async_copy(gkv, gk_h, out_sem.at[2 * HEADS + 1])
    gv_out = pltpu.make_async_copy(gvv, gv_h, out_sem.at[2 * HEADS + 2])
    gk_out.start()
    gv_out.start()

    for p in range(1, 4):
        ss_copy(p).wait_send()
        cc_copy(p).wait_send()
        ag_copy(0, p).wait_send()
        ag_copy(1, p).wait_send()
        for b in range(NB):
            kv_copy(b, p).wait_send()
    for k in range(1, 2 * ZS):
        gain_copy(k).wait_send()
    for p in range(4):
        for zt in range(ZS):
            cx_copy(p, zt).wait_send()

            @pl.when(z != zt)
            def _():
                right_copy(p, zt).wait_send()
    for c in outs + [gh_out, gk_out, gv_out]:
        c.wait()


def fused_body(hidden_in, norm_gain, key_weight, value_weight, queries, segments, cotangent):
    half = np.arange(HD // 2, dtype=np.float32) * np.float32(2.0 / HD)
    freq = np.power(np.float32(ROPE_BASE), -half).astype(np.float32)
    freq = jnp.asarray(np.concatenate([freq, freq])[None, :])
    vmem = pl.BlockSpec(memory_space=pltpu.VMEM)
    hbm = pl.BlockSpec(memory_space=pl.ANY)
    dma = pltpu.SemaphoreType.DMA
    V = pltpu.VMEM
    outs = pl.pallas_call(
        fused_kernel,
        out_shape=(
            jax.ShapeDtypeStruct((ROWS, HEADS * HD), BF16),
            jax.ShapeDtypeStruct((ROWS, FEAT), BF16),
            jax.ShapeDtypeStruct((ROWS, HEADS * HD), BF16),
            jax.ShapeDtypeStruct((SH, KVH * HD), F32),
            jax.ShapeDtypeStruct((SH, KVH * HD), F32),
            jax.ShapeDtypeStruct((1, SH), F32),
        ),
        in_specs=[hbm, vmem, hbm, hbm, hbm, vmem, hbm, vmem],
        out_specs=(hbm, hbm, hbm, hbm, hbm, vmem),
        scratch_shapes=[
            V((ROWS, FEAT), BF16),
            V((KVH, FEAT, KV), BF16),
            V((HEADS, ROWS, HD), BF16),
            V((HEADS, ROWS, HD), BF16),
            V((HEADS, ROWS, HD), BF16),
            V((ROWS, HD), F32),
            V((ROWS, HD), F32),
            V((ROWS, 1), F32),
            V((ROWS, 1), F32),
            V((ROWS, FEAT), BF16),
            V((FEAT, ROWS), BF16),
            V((4, 8, ROWS), F32),
            V((NB, 3, BLK, KV), KV_SEND),
            V((NB, 3, BLK, KV), KV_SEND),
            V((NB, BLK, KV), F32),
            V((ROWS, HD), BF16),
            V((ROWS, HD), BF16),
            V((ROWS, HD), F32),
            V((ROWS, HD), F32),
            V((HEADS, ROWS, HD), BF16),
            V((HEADS, ROWS, HD), BF16),
            V((KVH, ROWS, KV), BF16),
            V((ROWS, FEAT), F32),
            V((ROWS, 128), F32),
            V((4, 8, ROWS), F32),
            V((2 * ZS, 8, SH), F32),
            V((2 * ZS, 8, SH), F32),
            V((4, ZS, SH, KV), BF16),
            V((4, ZS, SH, KV), BF16),
            V((4, ZS, SH, KV), F32),
            V((4, ZS, SH, KV), BF16),
            V((4, ZS, SH, KV), BF16),
            V((4, ZS, SH, KV), BF16),
            V((SH, KVH * HD), F32),
            V((SH, KVH * HD), F32),
            V((ROWS, FEAT), BF16),
            dma((25,)), dma((2 * HEADS + 3,)),
            dma((3,)), dma((3,)),
            dma((NB, 3)), dma((NB, 3)),
            dma((2, 3)), dma((2, 3)),
            dma((3,)), dma((3,)),
            dma((2 * ZS,)), dma((2 * ZS,)),
            dma((4, ZS)), dma((4, ZS)),
            dma((4, ZS)), dma((4, ZS)), dma((4, ZS)),
        ],
        compiler_params=pltpu.CompilerParams(
            collective_id=0, has_side_effects=True, vmem_limit_bytes=56 * 1024 * 1024
        ),
        name="fused_block",
    )(
        hidden_in, norm_gain[None, :], key_weight, value_weight, queries, segments, cotangent,
        freq,
    )
    return outs[:5] + (outs[5][0],)


def solution(mesh):
    fused = (mesh.shape["dp"], mesh.shape["tensor"]) == (2 * ZS, TS)
    body = fused_body if fused else plain_body
    return jax.shard_map(
        body,
        mesh=mesh,
        in_specs=(
            P("dp", "tensor"),
            P("tensor"),
            P("tensor", None),
            P("tensor", None),
            P("dp", "tensor"),
            P("dp", None),
            P("dp", "tensor"),
        ),
        out_specs=(
            P("dp", "tensor"),
            P("dp", "tensor"),
            P("dp", "tensor"),
            P(("tensor", "dp"), None),
            P(("tensor", "dp"), None),
            P(("tensor", "dp")),
        ),
        check_vma=False,
    )
```

```python
import functools

import jax
import jax.numpy as jnp
import numpy as np
from jax import lax
from jax.experimental import pallas as pl
from jax.experimental.pallas import tpu as pltpu
from jax.sharding import PartitionSpec as P

D = 8192
HQ = 32
KVH = 4
HD = 128


ROPE_BASE = 500000.0


def angles(pos, head_size, ndim):
    half = head_size // 2
    freq = ROPE_BASE ** (-(jnp.arange(half).astype(jnp.float32) * 2.0 / head_size))
    angle = pos[:, None] * freq[None, :]
    shape = (pos.shape[0],) + (1,) * (ndim - 2) + (half,)
    return (jnp.cos(angle).reshape(shape), jnp.sin(angle).reshape(shape))


def rotate(vec, pos, sign):
    half = vec.shape[-1] // 2
    cosine, sine = angles(pos, vec.shape[-1], vec.ndim)
    first = vec[..., :half]
    second = vec[..., half:]
    return jnp.concatenate(
        [first * cosine - sign * second * sine, second * cosine + sign * first * sine], axis=-1
    )


def row_layout(seg):
    rows = seg.shape[0]
    index = jnp.arange(rows)
    same = seg[:, None] == seg[None, :]
    start = jnp.min(jnp.where(same, index[None, :], rows), axis=1)
    pos = (index - start).astype(jnp.float32)
    allowed = same & (index[None, :] <= index[:, None])
    return (pos, allowed)


def plain_body(hidden_in, norm_gain, key_weight, value_weight, queries, segments, cotangent):
    rows = hidden_in.shape[0]
    width = key_weight.shape[1]
    group = HQ // KVH
    scale = 1.0 / HD**0.5
    tens_size = lax.axis_size("tensor")
    tens_index = lax.axis_index("tensor")
    local_heads = queries.shape[1] // HD
    kv_count = max(local_heads // group, 1)
    repeat = min(local_heads, group)
    kv_first = tens_index * local_heads // group
    sharers = max(tens_size // KVH, 1)
    in_float = hidden_in.astype(jnp.float32)
    square_sum = lax.psum(jnp.sum(in_float * in_float, axis=1), "tensor")
    inv_rms = lax.rsqrt(square_sum / D + 1e-05)
    unit = in_float * inv_rms[:, None]
    normed = (unit * norm_gain[None, :]).astype(jnp.bfloat16)
    partial_value = jnp.stack(
        [
            jnp.dot(normed, key_weight, preferred_element_type=jnp.float32),
            jnp.dot(normed, value_weight, preferred_element_type=jnp.float32),
        ],
        axis=1,
    )
    kv_both = lax.psum(partial_value.reshape(rows, 2 * width), "tensor").astype(jnp.bfloat16)
    kv_heads = kv_both.reshape(rows, 2, KVH, HD)
    key_local = lax.dynamic_slice_in_dim(kv_heads[:, 0], kv_first, kv_count, 1)
    value_local = lax.dynamic_slice_in_dim(kv_heads[:, 1], kv_first, kv_count, 1)
    pos, allowed = row_layout(segments[0])
    query_four = queries.reshape(rows, kv_count, repeat, HD)
    q_rot = rotate(query_four.astype(jnp.float32), pos, 1.0).astype(jnp.bfloat16)
    k_rot = rotate(key_local.astype(jnp.float32), pos, 1.0).astype(jnp.bfloat16)
    scores = jnp.einsum("qcrd,kcd->crqk", q_rot, k_rot, preferred_element_type=jnp.float32) * scale
    scores = jnp.where(allowed[None, None], scores, -1e30)
    top = jnp.max(scores, axis=-1, keepdims=True)
    expo = jnp.exp(scores - top)
    probs = (expo / jnp.sum(expo, axis=-1, keepdims=True)).astype(jnp.bfloat16)
    attn_out = (
        jnp.einsum("crqk,kcd->qcrd", probs, value_local, preferred_element_type=jnp.float32)
        .astype(jnp.bfloat16)
        .reshape(rows, local_heads * HD)
    )
    cot_four = cotangent.reshape(rows, kv_count, repeat, HD)
    d_probs = jnp.einsum(
        "qcrd,kcd->crqk", cot_four, value_local, preferred_element_type=jnp.float32
    )
    prob_float = probs.astype(jnp.float32)
    delta = jnp.sum(prob_float * d_probs, axis=-1, keepdims=True)
    d_scores = (prob_float * (d_probs - delta) * scale).astype(jnp.bfloat16)
    d_qrot = jnp.einsum("crqk,kcd->qcrd", d_scores, k_rot, preferred_element_type=jnp.float32)
    grad_queries = rotate(d_qrot, pos, -1.0).astype(jnp.bfloat16).reshape(rows, local_heads * HD)
    d_krot = jnp.einsum("crqk,qcrd->kcd", d_scores, q_rot, preferred_element_type=jnp.float32)
    d_key_part = rotate(d_krot, pos, -1.0)
    d_value_part = jnp.einsum("crqk,qcrd->kcd", probs, cot_four, preferred_element_type=jnp.float32)
    grad_part = jnp.stack([d_key_part, d_value_part], axis=1)
    gathered = lax.all_gather(grad_part.astype(jnp.bfloat16), "tensor", axis=2, tiled=True).astype(
        grad_part.dtype
    )
    summed = jnp.sum(gathered.reshape(rows, 2, KVH, sharers, HD), axis=3)
    kv_grad = summed.astype(jnp.bfloat16).reshape(rows, 2, width)
    d_keys = kv_grad[:, 0]
    d_values = kv_grad[:, 1]
    d_normed = jnp.dot(d_keys, key_weight.T, preferred_element_type=jnp.float32) + jnp.dot(
        d_values, value_weight.T, preferred_element_type=jnp.float32
    )
    key_term = jnp.dot(normed.T, d_keys, preferred_element_type=jnp.float32)
    value_term = jnp.dot(normed.T, d_values, preferred_element_type=jnp.float32)
    gain_term = jnp.sum(d_normed * unit, axis=0)
    grad_key, grad_value, grad_gain = (
        lax.psum_scatter(
            key_term.astype(jnp.bfloat16), "dp", scatter_dimension=0, tiled=True
        ).astype(jnp.float32),
        lax.psum_scatter(
            value_term.astype(jnp.bfloat16), "dp", scatter_dimension=0, tiled=True
        ).astype(jnp.float32),
        lax.psum_scatter(
            gain_term.astype(jnp.bfloat16), "dp", scatter_dimension=0, tiled=True
        ).astype(jnp.float32),
    )
    d_unit = d_normed * norm_gain[None, :]
    corr = lax.psum(jnp.sum(d_unit * unit, axis=1), "tensor") / D
    grad_hidden = (inv_rms[:, None] * (d_unit - unit * corr[:, None])).astype(jnp.bfloat16)
    return (attn_out, grad_hidden, grad_queries, grad_key, grad_value, grad_gain)


ZS = 4
TS = 4
ROWS = 512
FEAT = 2048
BLK = 128
NB = ROWS // BLK
HEADS = HQ // TS
GH = 4
KV = 2 * HD
SH = FEAT // (2 * ZS)
MESH = pl.DeviceIdType.MESH
F32 = jnp.float32
BF16 = jnp.bfloat16


def dot_nn(a, b):
    return lax.dot_general(a, b, (((1,), (0,)), ((), ())), preferred_element_type=F32)


def dot_nt(a, b):
    return lax.dot_general(a, b, (((1,), (1,)), ((), ())), preferred_element_type=F32)


def dot_tn(a, b):
    return lax.dot_general(a, b, (((0,), (0,)), ((), ())), preferred_element_type=F32)


def eye_mask():
    return lax.broadcasted_iota(jnp.int32, (BLK, BLK), 0) == lax.broadcasted_iota(
        jnp.int32, (BLK, BLK), 1
    )


def col_to_row(col):
    return jnp.sum(jnp.where(eye_mask(), col, 0.0), axis=0, keepdims=True)


def row_to_col(row):
    return jnp.sum(jnp.where(eye_mask(), row, 0.0), axis=1, keepdims=True)


def swap_halves(vec):
    return pltpu.roll(vec, HD // 2, vec.ndim - 1)


def fused_kernel(
    hid_h, gain_h, kw_h, vw_h, q_h, seg_h, cot_h, freq_h,
    ao_h, gh_h, gq_h, gk_h, gv_h, gg_v,
    hid, w4, qs, cs, qr, cosv, sinv, segc, invc, normed, dkvt,
    gain_v, seg_v, freq_v, ss, ksend, vsend, krecv, vrecv, own_kv, krot, vals, dk_acc, dv_acc, ao, gq,
    dkv, du, corr_acc, cc, gsend, grecv,
    csend, crecv, own, zsend, zfl, zfr, gkv, gvv, gh,
    in_sem, out_sem, ss_s, ss_r, kv_s, kv_r, ag_s, ag_r, co_s, co_r,
    ga_s, ga_r, cx_s, cx_r, zs_s, zl_r, zr_r,
):
    dp = lax.axis_index("dp")
    t = lax.axis_index("tensor")
    z = dp // 2
    core = dp % 2
    other = 1 - core
    dp_other = dp + 1 - 2 * core
    peers = [t, t + 1 - 2 * (t % 2), (t + 2) % 4, 3 - t]

    def remote(src, dst, ssem, rsem, dev):
        return pltpu.make_async_remote_copy(
            src_ref=src, dst_ref=dst, send_sem=ssem, recv_sem=rsem,
            device_id=dev, device_id_type=MESH,
        )

    barrier = pltpu.get_barrier_semaphore()
    for p in range(1, 4):
        pl.semaphore_signal(barrier, inc=1, device_id=(dp, peers[p]), device_id_type=MESH)
    for k in range(1, 2 * ZS):
        pl.semaphore_signal(
            barrier, inc=1, device_id=((dp + k) % (2 * ZS), t), device_id_type=MESH
        )

    loads = [pltpu.make_async_copy(hid_h, hid, in_sem.at[0])]
    q_loads = [
        pltpu.make_async_copy(q_h.at[:, pl.ds(h * HD, HD)], qs.at[h], in_sem.at[1 + h])
        for h in range(HEADS)
    ]
    w_loads = []
    for h in range(KVH):
        w_loads.append(pltpu.make_async_copy(
            kw_h.at[:, pl.ds(h * HD, HD)], w4.at[h, :, pl.ds(0, HD)], in_sem.at[9 + 2 * h]))
        w_loads.append(pltpu.make_async_copy(
            vw_h.at[:, pl.ds(h * HD, HD)], w4.at[h, :, pl.ds(HD, HD)], in_sem.at[10 + 2 * h]))
    c_loads = [
        pltpu.make_async_copy(cot_h.at[:, pl.ds(h * HD, HD)], cs.at[h], in_sem.at[17 + h])
        for h in range(HEADS)
    ]
    small = [
        pltpu.make_async_copy(seg_h, seg_v, in_sem.at[25]),
        pltpu.make_async_copy(freq_h, freq_v, in_sem.at[26]),
        pltpu.make_async_copy(gain_h, gain_v, in_sem.at[27]),
    ]
    for c in loads + small + q_loads + w_loads + c_loads:
        c.start()

    loads[0].wait()
    for b in range(NB):
        x = hid[pl.ds(b * BLK, BLK), :].astype(F32)
        ss[0, :, pl.ds(b * BLK, BLK)] = jnp.broadcast_to(
            col_to_row(jnp.sum(x * x, axis=1, keepdims=True)), (8, BLK)
        )
    pl.semaphore_wait(barrier, 3 + 2 * ZS - 1)

    def ss_copy(p):
        return remote(ss.at[0], ss.at[p], ss_s.at[p - 1], ss_r.at[p - 1], (dp, peers[p]))

    for p in range(1, 4):
        ss_copy(p).start()

    for c in small:
        c.wait()
    segr = seg_v[...].astype(F32)
    for b in range(NB):
        rows = pl.ds(b * BLK, BLK)
        col = row_to_col(segr[:, b * BLK:(b + 1) * BLK])
        segc[rows, :] = col
        start = jnp.sum(jnp.where(segr < col, 1.0, 0.0), axis=1, keepdims=True)
        index = lax.broadcasted_iota(jnp.int32, (BLK, 1), 0).astype(F32) + float(b * BLK)
        angle = (index - start) * freq_v[...]
        lane = lax.broadcasted_iota(jnp.int32, (BLK, HD), 1)
        cosv[rows, :] = jnp.cos(angle)
        sinv[rows, :] = jnp.where(lane < HD // 2, -1.0, 1.0) * jnp.sin(angle)
    for p in range(1, 4):
        ss_copy(p).wait_recv()
    total = ss[0, 0:1, :] + ss[1, 0:1, :] + ss[2, 0:1, :] + ss[3, 0:1, :]
    inv_row = lax.rsqrt(total / D + 1e-05)
    for b in range(NB):
        invc[pl.ds(b * BLK, BLK), :] = row_to_col(inv_row[:, b * BLK:(b + 1) * BLK])
    for c in w_loads:
        c.wait()

    def k_copy(b, p):
        return remote(
            ksend.at[b, p - 1], krecv.at[b, p - 1], kv_s.at[0, b, p - 1], kv_r.at[0, b, p - 1],
            (dp, peers[p]),
        )

    def v_copy(b, p):
        return remote(
            vsend.at[b, p - 1], vrecv.at[b, p - 1], kv_s.at[1, b, p - 1], kv_r.at[1, b, p - 1],
            (dp, peers[p]),
        )

    for b in range(NB):
        rows = pl.ds(b * BLK, BLK)
        unit = hid[rows, :].astype(F32) * invc[rows, :]
        normed[rows, :] = (unit * gain_v[...]).astype(BF16)
        for p in (3, 1, 2, 0):
            part = dot_nn(normed[rows, :], w4[peers[p]])
            if p == 0:
                own_kv[b] = part
            else:
                ksend[b, p - 1] = part[:, :HD]
                k_copy(b, p).start()
                vsend[b, p - 1] = part[:, HD:].astype(BF16)
                v_copy(b, p).start()
    for c in q_loads:
        c.wait()

    def rot_query(h, carry):
        v = qs[h].astype(F32)
        qr[h] = (v * cosv[...] + swap_halves(v) * sinv[...]).astype(BF16)
        return carry

    lax.fori_loop(0, HEADS, rot_query, 0)

    for c in c_loads:
        c.wait()

    dk_acc[...] = jnp.zeros_like(dk_acc)
    dv_acc[...] = jnp.zeros_like(dv_acc)
    scale = 1.0 / HD**0.5

    def ag_copy(part, p):
        rows = pl.ds(0, BLK) if part == 0 else pl.ds(BLK, ROWS - BLK)
        return remote(
            dkv.at[t, rows], dkv.at[t, rows], ag_s.at[part, p - 1], ag_r.at[part, p - 1],
            (dp, peers[p]),
        )

    def ag_wait(part, p):
        rows = pl.ds(0, BLK) if part == 0 else pl.ds(BLK, ROWS - BLK)
        remote(
            dkv.at[peers[p], rows], dkv.at[peers[p], rows], ag_s.at[part, p - 1],
            ag_r.at[part, p - 1], (dp, peers[p]),
        ).wait_recv()

    def finish_grads(part):
        rows = pl.ds(0, BLK) if part == 0 else pl.ds(BLK, ROWS - BLK)
        dk = dk_acc[:, rows].T
        dkv[t, rows, pl.ds(0, HD)] = (
            dk * cosv[rows, :] - swap_halves(dk) * sinv[rows, :]
        ).astype(BF16)
        dkv[t, rows, pl.ds(HD, HD)] = dv_acc[:, rows].T.astype(BF16)
        for p in (1, 2, 3):
            ag_copy(part, p).start()

    for b in range(NB):
        rows = pl.ds(b * BLK, BLK)
        low = max(0, b - 2) * BLK
        width = (b + 1) * BLK - low
        window = pl.ds(low, width)
        for p in range(1, 4):
            k_copy(b, p).wait_recv()
            v_copy(b, p).wait_recv()
        key = own_kv[b, :, :HD]
        val = own_kv[b, :, HD:]
        for p in range(1, 4):
            key = key + krecv[b, p - 1]
            val = val + vrecv[b, p - 1].astype(F32)
        key = key.astype(BF16).astype(F32)
        krot[rows, :] = (key * cosv[rows, :] + swap_halves(key) * sinv[rows, :]).astype(BF16)
        vals[rows, :] = val.astype(BF16)
        q_index = lax.broadcasted_iota(jnp.int32, (BLK, width), 0) + b * BLK
        k_index = lax.broadcasted_iota(jnp.int32, (BLK, width), 1) + low
        same = segc[rows, :] == segr[:, low:low + width]
        bias = jnp.where(same & (k_index <= q_index), 0.0, -1e30)

        def group(g, carry):
            heads = pl.ds(g * GH, GH)
            qg = qr[heads, rows, :].reshape(GH * BLK, HD)
            cg = cs[heads, rows, :].reshape(GH * BLK, HD)
            kwin = krot[window, :]
            vwin = vals[window, :]
            s = dot_nt(qg, kwin).reshape(GH, BLK, width) * scale + bias[None]
            e = jnp.exp(s - jnp.max(s, axis=-1, keepdims=True))
            pb = (e * (1.0 / jnp.sum(e, axis=-1, keepdims=True))).astype(BF16)
            pf = pb.astype(F32)
            pb = pb.reshape(GH * BLK, width)
            ao[heads, rows, :] = dot_nn(pb, vwin).astype(BF16).reshape(GH, BLK, HD)
            dpr = dot_nt(cg, vwin).reshape(GH, BLK, width)
            delta = jnp.sum(pf * dpr, axis=-1, keepdims=True)
            ds = (pf * (dpr - delta) * scale).astype(BF16).reshape(GH * BLK, width)
            dq = dot_nn(ds, kwin).reshape(GH, BLK, HD)
            gq[heads, rows, :] = (
                dq * cosv[rows, :][None] - swap_halves(dq) * sinv[rows, :][None]
            ).astype(BF16)
            dk_acc[:, window] += dot_tn(qg, ds)
            dv_acc[:, window] += dot_tn(cg, pb)
            return carry

        lax.fori_loop(0, HEADS // GH, group, 0)
        if b == 2:
            finish_grads(0)
    finish_grads(1)

    outs = []
    for h in range(HEADS):
        outs.append(pltpu.make_async_copy(ao.at[h], ao_h.at[:, pl.ds(h * HD, HD)], out_sem.at[h]))
        outs.append(pltpu.make_async_copy(
            gq.at[h], gq_h.at[:, pl.ds(h * HD, HD)], out_sem.at[HEADS + h]))
    for c in outs:
        c.start()

    def cx_copy(p, zt):
        return remote(
            csend.at[p, zt], crecv.at[p, zt], cx_s.at[p, zt], cx_r.at[p, zt], (dp_other, t)
        )

    def partials(p):
        dkvt[...] = dkv[peers[p]].astype(F32).T.astype(BF16)
        for zt in (3, 0, 2, 1):
            far = normed[:, pl.ds(pl.multiple_of((2 * zt + other) * SH, SH), SH)]
            csend[p, zt] = dot_nn(dkvt[...], far).astype(BF16)
            cx_copy(p, zt).start()
        for zt in (3, 0, 2, 1):
            near = normed[:, pl.ds(pl.multiple_of((2 * zt + core) * SH, SH), SH)]
            own[p, zt] = dot_nn(dkvt[...], near)

    def pair_sums(p):
        for zt in (3, 0, 2, 1):
            cx_copy(p, zt).wait_recv()
            own[p, zt] = own[p, zt] + crecv[p, zt].astype(F32)

    def right_copy(p, zt):
        return remote(
            zsend.at[p, zt], zfl.at[p, zt], zs_s.at[p, zt], zl_r.at[p, zt], ((dp + 2) % (2 * ZS), t)
        )

    def left_copy(p, zt):
        return remote(
            zsend.at[p, zt], zfr.at[p, zt], zs_s.at[p, zt], zr_r.at[p, zt], ((dp + 2 * ZS - 2) % (2 * ZS), t)
        )

    def end_sends(p):
        @pl.when(z == 0)
        def _():
            for zt in range(ZS - 1, 0, -1):
                zsend[p, zt] = own[p, zt].astype(BF16)
                right_copy(p, zt).start()

        @pl.when(z == ZS - 1)
        def _():
            for zt in range(ZS - 1):
                zsend[p, zt] = own[p, zt].astype(BF16)
                left_copy(p, zt).start()

    def relay_right(p, zt):
        right_copy(p, zt).wait_recv()
        zsend[p, zt] = (own[p, zt] + zfl[p, zt].astype(F32)).astype(BF16)
        right_copy(p, zt).start()

    def relay_left(p, zt):
        left_copy(p, zt).wait_recv()
        zsend[p, zt] = (own[p, zt] + zfr[p, zt].astype(F32)).astype(BF16)
        left_copy(p, zt).start()

    def middle_sends(p):
        @pl.when(z == 1)
        def _():
            relay_right(p, 3)
            relay_right(p, 2)
            relay_left(p, 0)

        @pl.when(z == 2)
        def _():
            relay_left(p, 0)
            relay_left(p, 1)
            relay_right(p, 3)

    partials(0)
    pair_sums(0)
    end_sends(0)
    for p in range(1, 4):
        ag_wait(0, p)
        ag_wait(1, p)
        partials(p)
        pair_sums(p)
        end_sends(p)

    corr_acc[...] = jnp.zeros_like(corr_acc)

    def feature_chunk(f, carry):
        cols = pl.ds(pl.multiple_of(f * SH, SH), SH)
        dn = dot_nt(dkv[0], w4[0, cols, :])
        for h in range(1, KVH):
            dn = dn + dot_nt(dkv[h], w4[h, cols, :])
        unit = hid[:, cols].astype(F32) * invc[...]
        gsend[f] = jnp.sum((dn * unit).reshape(ROWS // 8, 8, SH), axis=0)
        dun = dn * gain_v[:, cols]
        du[:, cols] = dun
        w = dun * unit
        corr_acc[...] += w[:, :128] + w[:, 128:]
        return carry

    lax.fori_loop(0, 2 * ZS, feature_chunk, 0)
    for b in range(NB):
        rows = pl.ds(b * BLK, BLK)
        cc[0, :, rows] = jnp.broadcast_to(
            col_to_row(jnp.sum(corr_acc[rows, :], axis=1, keepdims=True)), (8, BLK)
        )

    def cc_copy(p):
        return remote(cc.at[0], cc.at[p], co_s.at[p - 1], co_r.at[p - 1], (dp, peers[p]))

    def gain_copy(k):
        to = (dp + k) % (2 * ZS)
        return remote(gsend.at[to], grecv.at[k], ga_s.at[k], ga_r.at[k], (to, t))

    for p in range(1, 4):
        cc_copy(p).start()
    for k in range(1, 2 * ZS):
        gain_copy(k).start()

    middle_sends(0)
    for p in range(1, 4):
        cc_copy(p).wait_recv()
    corr_row = (cc[0, 0:1, :] + cc[1, 0:1, :] + cc[2, 0:1, :] + cc[3, 0:1, :]) / D
    for b in range(NB):
        rows = pl.ds(b * BLK, BLK)
        corr = row_to_col(corr_row[:, b * BLK:(b + 1) * BLK])
        inv = invc[rows, :]
        unit = hid[rows, :].astype(F32) * inv
        gh[rows, :] = (inv * (du[rows, :] - unit * corr)).astype(BF16)
    gh_out = pltpu.make_async_copy(gh, gh_h, out_sem.at[2 * HEADS])
    gh_out.start()

    for p in range(1, 4):
        middle_sends(p)

    for k in range(1, 2 * ZS):
        gain_copy(k).wait_recv()
    gain_sum = gsend[dp]
    for k in range(1, 2 * ZS):
        gain_sum = gain_sum + grecv[k]
    gg_v[...] = jnp.sum(gain_sum, axis=0, keepdims=True)

    for p in range(4):
        for zt in range(ZS):
            @pl.when(z == zt)
            def _():
                res = own[p, zt]
                if zt > 0:
                    right_copy(p, zt).wait_recv()
                    res = res + zfl[p, zt].astype(F32)
                if zt < ZS - 1:
                    left_copy(p, zt).wait_recv()
                    res = res + zfr[p, zt].astype(F32)
                res = res.T
                cols = pl.ds(pl.multiple_of(peers[p] * HD, HD), HD)
                gkv[:, cols] = res[:, :HD]
                gvv[:, cols] = res[:, HD:]
    gk_out = pltpu.make_async_copy(gkv, gk_h, out_sem.at[2 * HEADS + 1])
    gv_out = pltpu.make_async_copy(gvv, gv_h, out_sem.at[2 * HEADS + 2])
    gk_out.start()
    gv_out.start()

    for p in range(1, 4):
        ss_copy(p).wait_send()
        cc_copy(p).wait_send()
        ag_copy(0, p).wait_send()
        ag_copy(1, p).wait_send()
        for b in range(NB):
            k_copy(b, p).wait_send()
            v_copy(b, p).wait_send()
    for k in range(1, 2 * ZS):
        gain_copy(k).wait_send()
    for p in range(4):
        for zt in range(ZS):
            cx_copy(p, zt).wait_send()

            @pl.when(z != zt)
            def _():
                right_copy(p, zt).wait_send()
    for c in outs + [gh_out, gk_out, gv_out]:
        c.wait()


def store_kernel(*refs):
    ins, outs, sem = refs[:6], refs[6:12], refs[12]
    copies = []
    for src, dst, cuts in zip(ins, outs, (2, 4, 2, 1, 1, 1)):
        step = src.shape[0] // cuts
        for k in range(cuts):
            rows = pl.ds(k * step, step)
            copies.append(pltpu.make_async_copy(src.at[rows], dst.at[rows], sem.at[len(copies)]))
    for c in copies:
        c.start()
    for c in copies:
        c.wait()


def store_outputs(arrays):
    hbm = pl.BlockSpec(memory_space=pl.ANY)
    return pl.pallas_call(
        store_kernel,
        out_shape=tuple(jax.ShapeDtypeStruct(a.shape, a.dtype) for a in arrays),
        in_specs=[hbm] * 6,
        out_specs=(hbm,) * 6,
        scratch_shapes=[pltpu.SemaphoreType.DMA((11,))],
        compiler_params=pltpu.CompilerParams(vmem_limit_bytes=58 * 1024 * 1024),
        name="store_outputs",
    )(*arrays)


def fused_body(hidden_in, norm_gain, key_weight, value_weight, queries, segments, cotangent):
    half = np.arange(HD // 2, dtype=np.float32) * np.float32(2.0 / HD)
    freq = np.power(np.float32(ROPE_BASE), -half).astype(np.float32)
    freq = jnp.asarray(np.concatenate([freq, freq])[None, :])
    vmem = pl.BlockSpec(memory_space=pltpu.VMEM)
    hbm = pl.BlockSpec(memory_space=pl.ANY)
    pinned = pl.BlockSpec(memory_space=pl.ANY)
    dma = pltpu.SemaphoreType.DMA
    V = pltpu.VMEM
    outs = pl.pallas_call(
        fused_kernel,
        out_shape=(
            jax.ShapeDtypeStruct((ROWS, HEADS * HD), BF16),
            jax.ShapeDtypeStruct((ROWS, FEAT), BF16),
            jax.ShapeDtypeStruct((ROWS, HEADS * HD), BF16),
            jax.ShapeDtypeStruct((SH, KVH * HD), F32),
            jax.ShapeDtypeStruct((SH, KVH * HD), F32),
            jax.ShapeDtypeStruct((1, SH), F32),
        ),
        in_specs=[pinned] * 8,
        out_specs=(hbm, hbm, hbm, hbm, hbm, vmem),
        scratch_shapes=[
            V((ROWS, FEAT), BF16),
            V((KVH, FEAT, KV), BF16),
            V((HEADS, ROWS, HD), BF16),
            V((HEADS, ROWS, HD), BF16),
            V((HEADS, ROWS, HD), BF16),
            V((ROWS, HD), F32),
            V((ROWS, HD), F32),
            V((ROWS, 1), F32),
            V((ROWS, 1), F32),
            V((ROWS, FEAT), BF16),
            V((KV, ROWS), BF16),
            V((1, FEAT), F32),
            V((1, ROWS), jnp.int32),
            V((1, HD), F32),
            V((4, 8, ROWS), F32),
            V((NB, 3, BLK, HD), F32),
            V((NB, 3, BLK, HD), BF16),
            V((NB, 3, BLK, HD), F32),
            V((NB, 3, BLK, HD), BF16),
            V((NB, BLK, KV), F32),
            V((ROWS, HD), BF16),
            V((ROWS, HD), BF16),
            V((HD, ROWS), F32),
            V((HD, ROWS), F32),
            V((HEADS, ROWS, HD), BF16),
            V((HEADS, ROWS, HD), BF16),
            V((KVH, ROWS, KV), BF16),
            V((ROWS, FEAT), F32),
            V((ROWS, 128), F32),
            V((4, 8, ROWS), F32),
            V((2 * ZS, 8, SH), F32),
            V((2 * ZS, 8, SH), F32),
            V((4, ZS, KV, SH), BF16),
            V((4, ZS, KV, SH), BF16),
            V((4, ZS, KV, SH), F32),
            V((4, ZS, KV, SH), BF16),
            V((4, ZS, KV, SH), BF16),
            V((4, ZS, KV, SH), BF16),
            V((SH, KVH * HD), F32),
            V((SH, KVH * HD), F32),
            V((ROWS, FEAT), BF16),
            dma((28,)), dma((2 * HEADS + 3,)),
            dma((3,)), dma((3,)),
            dma((2, NB, 3)), dma((2, NB, 3)),
            dma((2, 3)), dma((2, 3)),
            dma((3,)), dma((3,)),
            dma((2 * ZS,)), dma((2 * ZS,)),
            dma((4, ZS)), dma((4, ZS)),
            dma((4, ZS)), dma((4, ZS)), dma((4, ZS)),
        ],
        compiler_params=pltpu.CompilerParams(
            collective_id=0, has_side_effects=True, vmem_limit_bytes=58 * 1024 * 1024
        ),
        name="fused_block",
    )(
        hidden_in, norm_gain[None, :], key_weight, value_weight, queries, segments, cotangent,
        freq,
    )
    outs = store_outputs(outs)
    return outs[:5] + (outs[5][0],)


def solution(mesh):
    fused = (mesh.shape["dp"], mesh.shape["tensor"]) == (2 * ZS, TS)
    body = fused_body if fused else plain_body
    return jax.shard_map(
        body,
        mesh=mesh,
        in_specs=(
            P("dp", "tensor"),
            P("tensor"),
            P("tensor", None),
            P("tensor", None),
            P("dp", "tensor"),
            P("dp", None),
            P("dp", "tensor"),
        ),
        out_specs=(
            P("dp", "tensor"),
            P("dp", "tensor"),
            P("dp", "tensor"),
            P(("tensor", "dp"), None),
            P(("tensor", "dp"), None),
            P(("tensor", "dp")),
        ),
        check_vma=False,
    )
```

```python
import functools

import jax
import jax.numpy as jnp
import numpy as np
from jax import lax
from jax.experimental import pallas as pl
from jax.experimental.pallas import tpu as pltpu
from jax.sharding import PartitionSpec as P

D = 8192
HQ = 32
KVH = 4
HD = 128


ROPE_BASE = 500000.0


def angles(pos, head_size, ndim):
    half = head_size // 2
    freq = ROPE_BASE ** (-(jnp.arange(half).astype(jnp.float32) * 2.0 / head_size))
    angle = pos[:, None] * freq[None, :]
    shape = (pos.shape[0],) + (1,) * (ndim - 2) + (half,)
    return (jnp.cos(angle).reshape(shape), jnp.sin(angle).reshape(shape))


def rotate(vec, pos, sign):
    half = vec.shape[-1] // 2
    cosine, sine = angles(pos, vec.shape[-1], vec.ndim)
    first = vec[..., :half]
    second = vec[..., half:]
    return jnp.concatenate(
        [first * cosine - sign * second * sine, second * cosine + sign * first * sine], axis=-1
    )


def row_layout(seg):
    rows = seg.shape[0]
    index = jnp.arange(rows)
    same = seg[:, None] == seg[None, :]
    start = jnp.min(jnp.where(same, index[None, :], rows), axis=1)
    pos = (index - start).astype(jnp.float32)
    allowed = same & (index[None, :] <= index[:, None])
    return (pos, allowed)


def plain_body(hidden_in, norm_gain, key_weight, value_weight, queries, segments, cotangent):
    rows = hidden_in.shape[0]
    width = key_weight.shape[1]
    group = HQ // KVH
    scale = 1.0 / HD**0.5
    tens_size = lax.axis_size("tensor")
    tens_index = lax.axis_index("tensor")
    local_heads = queries.shape[1] // HD
    kv_count = max(local_heads // group, 1)
    repeat = min(local_heads, group)
    kv_first = tens_index * local_heads // group
    sharers = max(tens_size // KVH, 1)
    in_float = hidden_in.astype(jnp.float32)
    square_sum = lax.psum(jnp.sum(in_float * in_float, axis=1), "tensor")
    inv_rms = lax.rsqrt(square_sum / D + 1e-05)
    unit = in_float * inv_rms[:, None]
    normed = (unit * norm_gain[None, :]).astype(jnp.bfloat16)
    partial_value = jnp.stack(
        [
            jnp.dot(normed, key_weight, preferred_element_type=jnp.float32),
            jnp.dot(normed, value_weight, preferred_element_type=jnp.float32),
        ],
        axis=1,
    )
    kv_both = lax.psum(partial_value.reshape(rows, 2 * width), "tensor").astype(jnp.bfloat16)
    kv_heads = kv_both.reshape(rows, 2, KVH, HD)
    key_local = lax.dynamic_slice_in_dim(kv_heads[:, 0], kv_first, kv_count, 1)
    value_local = lax.dynamic_slice_in_dim(kv_heads[:, 1], kv_first, kv_count, 1)
    pos, allowed = row_layout(segments[0])
    query_four = queries.reshape(rows, kv_count, repeat, HD)
    q_rot = rotate(query_four.astype(jnp.float32), pos, 1.0).astype(jnp.bfloat16)
    k_rot = rotate(key_local.astype(jnp.float32), pos, 1.0).astype(jnp.bfloat16)
    scores = jnp.einsum("qcrd,kcd->crqk", q_rot, k_rot, preferred_element_type=jnp.float32) * scale
    scores = jnp.where(allowed[None, None], scores, -1e30)
    top = jnp.max(scores, axis=-1, keepdims=True)
    expo = jnp.exp(scores - top)
    probs = (expo / jnp.sum(expo, axis=-1, keepdims=True)).astype(jnp.bfloat16)
    attn_out = (
        jnp.einsum("crqk,kcd->qcrd", probs, value_local, preferred_element_type=jnp.float32)
        .astype(jnp.bfloat16)
        .reshape(rows, local_heads * HD)
    )
    cot_four = cotangent.reshape(rows, kv_count, repeat, HD)
    d_probs = jnp.einsum(
        "qcrd,kcd->crqk", cot_four, value_local, preferred_element_type=jnp.float32
    )
    prob_float = probs.astype(jnp.float32)
    delta = jnp.sum(prob_float * d_probs, axis=-1, keepdims=True)
    d_scores = (prob_float * (d_probs - delta) * scale).astype(jnp.bfloat16)
    d_qrot = jnp.einsum("crqk,kcd->qcrd", d_scores, k_rot, preferred_element_type=jnp.float32)
    grad_queries = rotate(d_qrot, pos, -1.0).astype(jnp.bfloat16).reshape(rows, local_heads * HD)
    d_krot = jnp.einsum("crqk,qcrd->kcd", d_scores, q_rot, preferred_element_type=jnp.float32)
    d_key_part = rotate(d_krot, pos, -1.0)
    d_value_part = jnp.einsum("crqk,qcrd->kcd", probs, cot_four, preferred_element_type=jnp.float32)
    grad_part = jnp.stack([d_key_part, d_value_part], axis=1)
    gathered = lax.all_gather(grad_part.astype(jnp.bfloat16), "tensor", axis=2, tiled=True).astype(
        grad_part.dtype
    )
    summed = jnp.sum(gathered.reshape(rows, 2, KVH, sharers, HD), axis=3)
    kv_grad = summed.astype(jnp.bfloat16).reshape(rows, 2, width)
    d_keys = kv_grad[:, 0]
    d_values = kv_grad[:, 1]
    d_normed = jnp.dot(d_keys, key_weight.T, preferred_element_type=jnp.float32) + jnp.dot(
        d_values, value_weight.T, preferred_element_type=jnp.float32
    )
    key_term = jnp.dot(normed.T, d_keys, preferred_element_type=jnp.float32)
    value_term = jnp.dot(normed.T, d_values, preferred_element_type=jnp.float32)
    gain_term = jnp.sum(d_normed * unit, axis=0)
    grad_key, grad_value, grad_gain = (
        lax.psum_scatter(
            key_term.astype(jnp.bfloat16), "dp", scatter_dimension=0, tiled=True
        ).astype(jnp.float32),
        lax.psum_scatter(
            value_term.astype(jnp.bfloat16), "dp", scatter_dimension=0, tiled=True
        ).astype(jnp.float32),
        lax.psum_scatter(
            gain_term.astype(jnp.bfloat16), "dp", scatter_dimension=0, tiled=True
        ).astype(jnp.float32),
    )
    d_unit = d_normed * norm_gain[None, :]
    corr = lax.psum(jnp.sum(d_unit * unit, axis=1), "tensor") / D
    grad_hidden = (inv_rms[:, None] * (d_unit - unit * corr[:, None])).astype(jnp.bfloat16)
    return (attn_out, grad_hidden, grad_queries, grad_key, grad_value, grad_gain)


ZS = 4
TS = 4
ROWS = 512
FEAT = 2048
BLK = 128
NB = ROWS // BLK
HEADS = HQ // TS
GH = 4
KV = 2 * HD
SH = FEAT // (2 * ZS)
MESH = pl.DeviceIdType.MESH
F32 = jnp.float32
BF16 = jnp.bfloat16


def dot_nn(a, b):
    return lax.dot_general(a, b, (((1,), (0,)), ((), ())), preferred_element_type=F32)


def dot_nt(a, b):
    return lax.dot_general(a, b, (((1,), (1,)), ((), ())), preferred_element_type=F32)


def dot_tn(a, b):
    return lax.dot_general(a, b, (((0,), (0,)), ((), ())), preferred_element_type=F32)


def eye_mask():
    return lax.broadcasted_iota(jnp.int32, (BLK, BLK), 0) == lax.broadcasted_iota(
        jnp.int32, (BLK, BLK), 1
    )


def col_to_row(col):
    return jnp.sum(jnp.where(eye_mask(), col, 0.0), axis=0, keepdims=True)


def row_to_col(row):
    return jnp.sum(jnp.where(eye_mask(), row, 0.0), axis=1, keepdims=True)


def swap_halves(vec):
    return pltpu.roll(vec, HD // 2, vec.ndim - 1)


def fused_kernel(
    hid_h, gain_h, kw_h, vw_h, q_h, seg_h, cot_h, freq_h,
    ao_h, gh_h, gq_h, gk_h, gv_h, gg_v,
    hid, w4, qs, cs, qr, cosv, sinv, segc, invc, normed, dkvt,
    gain_v, seg_v, freq_v, ss, ksend, vsend, krecv, vrecv, own_kv, krot, vals, dk_acc, dv_acc, ao, gq,
    dkv, du, corr_acc, cc, gsend, grecv,
    csend, crecv, own, zsend, zfl, zfr, gkv, gvv, gh,
    in_sem, out_sem, ss_s, ss_r, kv_s, kv_r, ag_s, ag_r, co_s, co_r,
    ga_s, ga_r, cx_s, cx_r, zs_s, zl_r, zr_r,
):
    dp = lax.axis_index("dp")
    t = lax.axis_index("tensor")
    z = dp // 2
    core = dp % 2
    other = 1 - core
    dp_other = dp + 1 - 2 * core
    peers = [t, t + 1 - 2 * (t % 2), (t + 2) % 4, 3 - t]

    def remote(src, dst, ssem, rsem, dev):
        return pltpu.make_async_remote_copy(
            src_ref=src, dst_ref=dst, send_sem=ssem, recv_sem=rsem,
            device_id=dev, device_id_type=MESH,
        )

    barrier = pltpu.get_barrier_semaphore()
    for p in range(1, 4):
        pl.semaphore_signal(barrier, inc=1, device_id=(dp, peers[p]), device_id_type=MESH)
    for k in range(1, 2 * ZS):
        pl.semaphore_signal(
            barrier, inc=1, device_id=((dp + k) % (2 * ZS), t), device_id_type=MESH
        )

    loads = [pltpu.make_async_copy(hid_h, hid, in_sem.at[0])]
    q_loads = [
        pltpu.make_async_copy(q_h.at[:, pl.ds(h * HD, HD)], qs.at[h], in_sem.at[1 + h])
        for h in range(HEADS)
    ]
    w_loads = []
    for h in range(KVH):
        w_loads.append(pltpu.make_async_copy(
            kw_h.at[:, pl.ds(h * HD, HD)], w4.at[h, :, pl.ds(0, HD)], in_sem.at[9 + 2 * h]))
        w_loads.append(pltpu.make_async_copy(
            vw_h.at[:, pl.ds(h * HD, HD)], w4.at[h, :, pl.ds(HD, HD)], in_sem.at[10 + 2 * h]))
    c_loads = [
        pltpu.make_async_copy(cot_h.at[:, pl.ds(h * HD, HD)], cs.at[h], in_sem.at[17 + h])
        for h in range(HEADS)
    ]
    small = [
        pltpu.make_async_copy(seg_h, seg_v, in_sem.at[25]),
        pltpu.make_async_copy(freq_h, freq_v, in_sem.at[26]),
        pltpu.make_async_copy(gain_h, gain_v, in_sem.at[27]),
    ]
    for c in loads + small + q_loads + w_loads + c_loads:
        c.start()

    loads[0].wait()
    for b in range(NB):
        x = hid[pl.ds(b * BLK, BLK), :].astype(F32)
        ss[0, :, pl.ds(b * BLK, BLK)] = jnp.broadcast_to(
            col_to_row(jnp.sum(x * x, axis=1, keepdims=True)), (8, BLK)
        )
    pl.semaphore_wait(barrier, 3 + 2 * ZS - 1)

    def ss_copy(p):
        return remote(ss.at[0], ss.at[p], ss_s.at[p - 1], ss_r.at[p - 1], (dp, peers[p]))

    for p in range(1, 4):
        ss_copy(p).start()

    for c in small:
        c.wait()
    segr = seg_v[...].astype(F32)
    for b in range(NB):
        rows = pl.ds(b * BLK, BLK)
        col = row_to_col(segr[:, b * BLK:(b + 1) * BLK])
        segc[rows, :] = col
        start = jnp.sum(jnp.where(segr < col, 1.0, 0.0), axis=1, keepdims=True)
        index = lax.broadcasted_iota(jnp.int32, (BLK, 1), 0).astype(F32) + float(b * BLK)
        angle = (index - start) * freq_v[...]
        lane = lax.broadcasted_iota(jnp.int32, (BLK, HD), 1)
        cosv[rows, :] = jnp.cos(angle)
        sinv[rows, :] = jnp.where(lane < HD // 2, -1.0, 1.0) * jnp.sin(angle)
    for p in range(1, 4):
        ss_copy(p).wait_recv()
    total = ss[0, 0:1, :] + ss[1, 0:1, :] + ss[2, 0:1, :] + ss[3, 0:1, :]
    inv_row = lax.rsqrt(total / D + 1e-05)
    for b in range(NB):
        invc[pl.ds(b * BLK, BLK), :] = row_to_col(inv_row[:, b * BLK:(b + 1) * BLK])
    for c in w_loads:
        c.wait()

    def k_copy(b, p):
        return remote(
            ksend.at[b, p - 1], krecv.at[b, p - 1], kv_s.at[0, b, p - 1], kv_r.at[0, b, p - 1],
            (dp, peers[p]),
        )

    def v_copy(b, p):
        return remote(
            vsend.at[b, p - 1], vrecv.at[b, p - 1], kv_s.at[1, b, p - 1], kv_r.at[1, b, p - 1],
            (dp, peers[p]),
        )

    for b in range(NB):
        rows = pl.ds(b * BLK, BLK)
        unit = hid[rows, :].astype(F32) * invc[rows, :]
        normed[rows, :] = (unit * gain_v[...]).astype(BF16)
        for p in (3, 1, 2, 0):
            part = dot_nn(normed[rows, :], w4[peers[p]])
            if p == 0:
                own_kv[b] = part
            else:
                ksend[b, p - 1] = part[:, :HD]
                k_copy(b, p).start()
                vsend[b, p - 1] = part[:, HD:].astype(BF16)
                v_copy(b, p).start()
    for c in q_loads:
        c.wait()

    def rot_query(h, carry):
        v = qs[h].astype(F32)
        qr[h] = (v * cosv[...] + swap_halves(v) * sinv[...]).astype(BF16)
        return carry

    lax.fori_loop(0, HEADS, rot_query, 0)

    for c in c_loads:
        c.wait()

    dk_acc[...] = jnp.zeros_like(dk_acc)
    dv_acc[...] = jnp.zeros_like(dv_acc)
    scale = 1.0 / HD**0.5

    def ag_copy(part, p):
        rows = pl.ds(0, BLK) if part == 0 else pl.ds(BLK, ROWS - BLK)
        return remote(
            dkv.at[t, rows], dkv.at[t, rows], ag_s.at[part, p - 1], ag_r.at[part, p - 1],
            (dp, peers[p]),
        )

    def ag_wait(part, p):
        rows = pl.ds(0, BLK) if part == 0 else pl.ds(BLK, ROWS - BLK)
        remote(
            dkv.at[peers[p], rows], dkv.at[peers[p], rows], ag_s.at[part, p - 1],
            ag_r.at[part, p - 1], (dp, peers[p]),
        ).wait_recv()

    def finish_grads(part):
        rows = pl.ds(0, BLK) if part == 0 else pl.ds(BLK, ROWS - BLK)
        dk = dk_acc[:, rows].T
        dkv[t, rows, pl.ds(0, HD)] = (
            dk * cosv[rows, :] - swap_halves(dk) * sinv[rows, :]
        ).astype(BF16)
        dkv[t, rows, pl.ds(HD, HD)] = dv_acc[:, rows].T.astype(BF16)
        for p in (1, 2, 3):
            ag_copy(part, p).start()

    for b in range(NB):
        rows = pl.ds(b * BLK, BLK)
        low = max(0, b - 2) * BLK
        width = (b + 1) * BLK - low
        window = pl.ds(low, width)
        for p in range(1, 4):
            k_copy(b, p).wait_recv()
            v_copy(b, p).wait_recv()
        key = own_kv[b, :, :HD]
        val = own_kv[b, :, HD:]
        for p in range(1, 4):
            key = key + krecv[b, p - 1]
            val = val + vrecv[b, p - 1].astype(F32)
        key = key.astype(BF16).astype(F32)
        krot[rows, :] = (key * cosv[rows, :] + swap_halves(key) * sinv[rows, :]).astype(BF16)
        vals[rows, :] = val.astype(BF16)
        q_index = lax.broadcasted_iota(jnp.int32, (BLK, width), 0) + b * BLK
        k_index = lax.broadcasted_iota(jnp.int32, (BLK, width), 1) + low
        same = segc[rows, :] == segr[:, low:low + width]
        bias = jnp.where(same & (k_index <= q_index), 0.0, -1e30)

        def group(g, carry):
            heads = pl.ds(g * GH, GH)
            qg = qr[heads, rows, :].reshape(GH * BLK, HD)
            cg = cs[heads, rows, :].reshape(GH * BLK, HD)
            kwin = krot[window, :]
            vwin = vals[window, :]
            s = dot_nt(qg, kwin).reshape(GH, BLK, width) * scale + bias[None]
            e = jnp.exp(s - jnp.max(s, axis=-1, keepdims=True))
            pb = (e * (1.0 / jnp.sum(e, axis=-1, keepdims=True))).astype(BF16)
            pf = pb.astype(F32)
            pb = pb.reshape(GH * BLK, width)
            ao[heads, rows, :] = dot_nn(pb, vwin).astype(BF16).reshape(GH, BLK, HD)
            dpr = dot_nt(cg, vwin).reshape(GH, BLK, width)
            delta = jnp.sum(pf * dpr, axis=-1, keepdims=True)
            ds = (pf * (dpr - delta) * scale).astype(BF16).reshape(GH * BLK, width)
            dq = dot_nn(ds, kwin).reshape(GH, BLK, HD)
            gq[heads, rows, :] = (
                dq * cosv[rows, :][None] - swap_halves(dq) * sinv[rows, :][None]
            ).astype(BF16)
            dk_acc[:, window] += dot_tn(qg, ds)
            dv_acc[:, window] += dot_tn(cg, pb)
            return carry

        lax.fori_loop(0, HEADS // GH, group, 0)
        if b == 2:
            finish_grads(0)
    finish_grads(1)

    outs = []
    for h in range(HEADS):
        outs.append(pltpu.make_async_copy(ao.at[h], ao_h.at[:, pl.ds(h * HD, HD)], out_sem.at[h]))
        outs.append(pltpu.make_async_copy(
            gq.at[h], gq_h.at[:, pl.ds(h * HD, HD)], out_sem.at[HEADS + h]))
    for c in outs:
        c.start()

    def cx_copy(p, zt):
        return remote(
            csend.at[p, zt], crecv.at[p, zt], cx_s.at[p, zt], cx_r.at[p, zt], (dp_other, t)
        )

    def partials(p):
        dkvt[...] = dkv[peers[p]].astype(F32).T.astype(BF16)
        for zt in (3, 0, 2, 1):
            far = normed[:, pl.ds(pl.multiple_of((2 * zt + other) * SH, SH), SH)]
            csend[p, zt] = dot_nn(dkvt[...], far).astype(BF16)
            cx_copy(p, zt).start()
        for zt in (3, 0, 2, 1):
            near = normed[:, pl.ds(pl.multiple_of((2 * zt + core) * SH, SH), SH)]
            own[p, zt] = dot_nn(dkvt[...], near)

    def pair_sums(p):
        for zt in (3, 0, 2, 1):
            cx_copy(p, zt).wait_recv()
            own[p, zt] = own[p, zt] + crecv[p, zt].astype(F32)

    def right_copy(p, zt):
        return remote(
            zsend.at[p, zt], zfl.at[p, zt], zs_s.at[p, zt], zl_r.at[p, zt], ((dp + 2) % (2 * ZS), t)
        )

    def left_copy(p, zt):
        return remote(
            zsend.at[p, zt], zfr.at[p, zt], zs_s.at[p, zt], zr_r.at[p, zt], ((dp + 2 * ZS - 2) % (2 * ZS), t)
        )

    def end_sends(p):
        @pl.when(z == 0)
        def _():
            for zt in range(ZS - 1, 0, -1):
                zsend[p, zt] = own[p, zt].astype(BF16)
                right_copy(p, zt).start()

        @pl.when(z == ZS - 1)
        def _():
            for zt in range(ZS - 1):
                zsend[p, zt] = own[p, zt].astype(BF16)
                left_copy(p, zt).start()

    def relay_right(p, zt):
        right_copy(p, zt).wait_recv()
        zsend[p, zt] = (own[p, zt] + zfl[p, zt].astype(F32)).astype(BF16)
        right_copy(p, zt).start()

    def relay_left(p, zt):
        left_copy(p, zt).wait_recv()
        zsend[p, zt] = (own[p, zt] + zfr[p, zt].astype(F32)).astype(BF16)
        left_copy(p, zt).start()

    def middle_sends(p):
        @pl.when(z == 1)
        def _():
            relay_right(p, 3)
            relay_right(p, 2)
            relay_left(p, 0)

        @pl.when(z == 2)
        def _():
            relay_left(p, 0)
            relay_left(p, 1)
            relay_right(p, 3)

    partials(0)
    pair_sums(0)
    end_sends(0)
    for p in range(1, 4):
        ag_wait(0, p)
        ag_wait(1, p)
        partials(p)
        pair_sums(p)
        end_sends(p)

    corr_acc[...] = jnp.zeros_like(corr_acc)

    def feature_chunk(f, carry):
        cols = pl.ds(pl.multiple_of(f * SH, SH), SH)
        dn = dot_nt(dkv[0], w4[0, cols, :])
        for h in range(1, KVH):
            dn = dn + dot_nt(dkv[h], w4[h, cols, :])
        unit = hid[:, cols].astype(F32) * invc[...]
        gsend[f] = jnp.sum((dn * unit).reshape(ROWS // 8, 8, SH), axis=0)
        dun = dn * gain_v[:, cols]
        du[:, cols] = dun
        w = dun * unit
        corr_acc[...] += w[:, :128] + w[:, 128:]
        return carry

    lax.fori_loop(0, 2 * ZS, feature_chunk, 0)
    for b in range(NB):
        rows = pl.ds(b * BLK, BLK)
        cc[0, :, rows] = jnp.broadcast_to(
            col_to_row(jnp.sum(corr_acc[rows, :], axis=1, keepdims=True)), (8, BLK)
        )

    def cc_copy(p):
        return remote(cc.at[0], cc.at[p], co_s.at[p - 1], co_r.at[p - 1], (dp, peers[p]))

    def gain_copy(k):
        to = (dp + k) % (2 * ZS)
        return remote(gsend.at[to], grecv.at[k], ga_s.at[k], ga_r.at[k], (to, t))

    for p in range(1, 4):
        cc_copy(p).start()
    for k in range(1, 2 * ZS):
        gain_copy(k).start()

    middle_sends(0)
    for p in range(1, 4):
        cc_copy(p).wait_recv()
    corr_row = (cc[0, 0:1, :] + cc[1, 0:1, :] + cc[2, 0:1, :] + cc[3, 0:1, :]) / D
    for b in range(NB):
        rows = pl.ds(b * BLK, BLK)
        corr = row_to_col(corr_row[:, b * BLK:(b + 1) * BLK])
        inv = invc[rows, :]
        unit = hid[rows, :].astype(F32) * inv
        gh[rows, :] = (inv * (du[rows, :] - unit * corr)).astype(BF16)
    gh_out = pltpu.make_async_copy(gh, gh_h, out_sem.at[2 * HEADS])
    gh_out.start()

    for p in range(1, 4):
        middle_sends(p)

    for k in range(1, 2 * ZS):
        gain_copy(k).wait_recv()
    gain_sum = gsend[dp]
    for k in range(1, 2 * ZS):
        gain_sum = gain_sum + grecv[k]
    gg_v[...] = jnp.sum(gain_sum, axis=0, keepdims=True)

    for p in range(4):
        for zt in range(ZS):
            @pl.when(z == zt)
            def _():
                res = own[p, zt]
                if zt > 0:
                    right_copy(p, zt).wait_recv()
                    res = res + zfl[p, zt].astype(F32)
                if zt < ZS - 1:
                    left_copy(p, zt).wait_recv()
                    res = res + zfr[p, zt].astype(F32)
                res = res.T
                cols = pl.ds(pl.multiple_of(peers[p] * HD, HD), HD)
                gkv[:, cols] = res[:, :HD]
                gvv[:, cols] = res[:, HD:]
    gk_out = pltpu.make_async_copy(gkv, gk_h, out_sem.at[2 * HEADS + 1])
    gv_out = pltpu.make_async_copy(gvv, gv_h, out_sem.at[2 * HEADS + 2])
    gk_out.start()
    gv_out.start()

    for p in range(1, 4):
        ss_copy(p).wait_send()
        cc_copy(p).wait_send()
        ag_copy(0, p).wait_send()
        ag_copy(1, p).wait_send()
        for b in range(NB):
            k_copy(b, p).wait_send()
            v_copy(b, p).wait_send()
    for k in range(1, 2 * ZS):
        gain_copy(k).wait_send()
    for p in range(4):
        for zt in range(ZS):
            cx_copy(p, zt).wait_send()

            @pl.when(z != zt)
            def _():
                right_copy(p, zt).wait_send()
    for c in outs + [gh_out, gk_out, gv_out]:
        c.wait()


def store_kernel(*refs):
    ins, outs, bufs, in_sem, out_sem = refs[:6], refs[6:12], refs[12:18], refs[18], refs[19]
    reads, writes = [], []
    for src, buf, dst, cuts in zip(ins, bufs, outs, (2, 4, 2, 1, 1, 1)):
        step = src.shape[0] // cuts
        for k in range(cuts):
            rows = pl.ds(k * step, step)
            n = len(reads)
            reads.append(pltpu.make_async_copy(src.at[rows], buf.at[rows], in_sem.at[n]))
            writes.append(pltpu.make_async_copy(buf.at[rows], dst.at[rows], out_sem.at[n]))
    for c in reads:
        c.start()
    for r, w in zip(reads, writes):
        r.wait()
        w.start()
    for w in writes:
        w.wait()


def store_outputs(arrays):
    hbm = pl.BlockSpec(memory_space=pl.ANY)
    return pl.pallas_call(
        store_kernel,
        out_shape=tuple(jax.ShapeDtypeStruct(a.shape, a.dtype) for a in arrays),
        in_specs=[hbm] * 6,
        out_specs=(hbm,) * 6,
        scratch_shapes=[pltpu.VMEM(a.shape, a.dtype) for a in arrays]
        + [pltpu.SemaphoreType.DMA((11,)), pltpu.SemaphoreType.DMA((11,))],
        compiler_params=pltpu.CompilerParams(vmem_limit_bytes=58 * 1024 * 1024),
        name="store_outputs",
    )(*arrays)


def fused_body(hidden_in, norm_gain, key_weight, value_weight, queries, segments, cotangent):
    half = np.arange(HD // 2, dtype=np.float32) * np.float32(2.0 / HD)
    freq = np.power(np.float32(ROPE_BASE), -half).astype(np.float32)
    freq = jnp.asarray(np.concatenate([freq, freq])[None, :])
    vmem = pl.BlockSpec(memory_space=pltpu.VMEM)
    hbm = pl.BlockSpec(memory_space=pl.ANY)
    pinned = pl.BlockSpec(memory_space=pl.ANY)
    dma = pltpu.SemaphoreType.DMA
    V = pltpu.VMEM
    outs = pl.pallas_call(
        fused_kernel,
        out_shape=(
            jax.ShapeDtypeStruct((ROWS, HEADS * HD), BF16),
            jax.ShapeDtypeStruct((ROWS, FEAT), BF16),
            jax.ShapeDtypeStruct((ROWS, HEADS * HD), BF16),
            jax.ShapeDtypeStruct((SH, KVH * HD), F32),
            jax.ShapeDtypeStruct((SH, KVH * HD), F32),
            jax.ShapeDtypeStruct((1, SH), F32),
        ),
        in_specs=[pinned] * 8,
        out_specs=(hbm, hbm, hbm, hbm, hbm, vmem),
        scratch_shapes=[
            V((ROWS, FEAT), BF16),
            V((KVH, FEAT, KV), BF16),
            V((HEADS, ROWS, HD), BF16),
            V((HEADS, ROWS, HD), BF16),
            V((HEADS, ROWS, HD), BF16),
            V((ROWS, HD), F32),
            V((ROWS, HD), F32),
            V((ROWS, 1), F32),
            V((ROWS, 1), F32),
            V((ROWS, FEAT), BF16),
            V((KV, ROWS), BF16),
            V((1, FEAT), F32),
            V((1, ROWS), jnp.int32),
            V((1, HD), F32),
            V((4, 8, ROWS), F32),
            V((NB, 3, BLK, HD), F32),
            V((NB, 3, BLK, HD), BF16),
            V((NB, 3, BLK, HD), F32),
            V((NB, 3, BLK, HD), BF16),
            V((NB, BLK, KV), F32),
            V((ROWS, HD), BF16),
            V((ROWS, HD), BF16),
            V((HD, ROWS), F32),
            V((HD, ROWS), F32),
            V((HEADS, ROWS, HD), BF16),
            V((HEADS, ROWS, HD), BF16),
            V((KVH, ROWS, KV), BF16),
            V((ROWS, FEAT), F32),
            V((ROWS, 128), F32),
            V((4, 8, ROWS), F32),
            V((2 * ZS, 8, SH), F32),
            V((2 * ZS, 8, SH), F32),
            V((4, ZS, KV, SH), BF16),
            V((4, ZS, KV, SH), BF16),
            V((4, ZS, KV, SH), F32),
            V((4, ZS, KV, SH), BF16),
            V((4, ZS, KV, SH), BF16),
            V((4, ZS, KV, SH), BF16),
            V((SH, KVH * HD), F32),
            V((SH, KVH * HD), F32),
            V((ROWS, FEAT), BF16),
            dma((28,)), dma((2 * HEADS + 3,)),
            dma((3,)), dma((3,)),
            dma((2, NB, 3)), dma((2, NB, 3)),
            dma((2, 3)), dma((2, 3)),
            dma((3,)), dma((3,)),
            dma((2 * ZS,)), dma((2 * ZS,)),
            dma((4, ZS)), dma((4, ZS)),
            dma((4, ZS)), dma((4, ZS)), dma((4, ZS)),
        ],
        compiler_params=pltpu.CompilerParams(
            collective_id=0, has_side_effects=True, vmem_limit_bytes=58 * 1024 * 1024
        ),
        name="fused_block",
    )(
        hidden_in, norm_gain[None, :], key_weight, value_weight, queries, segments, cotangent,
        freq,
    )
    outs = store_outputs(outs)
    return outs[:5] + (outs[5][0],)


def solution(mesh):
    fused = (mesh.shape["dp"], mesh.shape["tensor"]) == (2 * ZS, TS)
    body = fused_body if fused else plain_body
    return jax.shard_map(
        body,
        mesh=mesh,
        in_specs=(
            P("dp", "tensor"),
            P("tensor"),
            P("tensor", None),
            P("tensor", None),
            P("dp", "tensor"),
            P("dp", None),
            P("dp", "tensor"),
        ),
        out_specs=(
            P("dp", "tensor"),
            P("dp", "tensor"),
            P("dp", "tensor"),
            P(("tensor", "dp"), None),
            P(("tensor", "dp"), None),
            P(("tensor", "dp")),
        ),
        check_vma=False,
    )
```
